128 devices in a mesh: ctx: 8 (over x, core), dp: 16 (over y, z).
Axes of the slice: x: 4, y: 4, z: 4, core: 2. Of those that a mesh axis runs over, the one named last changes fastest.
Arguments:
- query: bfloat16 [16, 1024, 64, 192], P('dp', 'ctx'), may hold values from -48 to 48
- latent: bfloat16 [16, 1024, 576], P('dp', 'ctx'), may hold values from -6 to 6
- doc_lengths: int32 [16, 8], P('dp'), may hold values from 1 to 256, 1024 in all within a row
- w_kv: bfloat16 [16384, 512], replicated, may hold values from -0.25 to 0.25
- grad_out: bfloat16 [16, 1024, 64, 128], P('dp', 'ctx'), may hold values from -6 to 6
Outputs:
- d_query: bfloat16 [16, 1024, 64, 192], P('dp', 'ctx')
- d_latent: bfloat16 [16, 1024, 576], P('dp', 'ctx')
- d_w_kv: float32 [16384, 512], P(('ctx', 'dp'))
The draws below stay inside these ranges and needn't reach their ends.
Inputs may be any that keep to these rules, and one draw needn't show every extreme that they name: `doc_lengths`: each row of 8 lengths sums to 1024; the longest document of every row has exactly 256 positions.
All inputs are finite; a program needn't handle non-finite values.
Results may differ from the reference program's by a relative error of at most 0.022.
Values may be sent and summed in bfloat16 or wider, within the bound.
No kernel may reach another device: no remote copies, remote signals or barrier semaphores. Data moves between devices by JAX's collectives and lax.ppermute only.
A program may use at most 256 MiB of HBM per device.

```python
import math
import jax
import jax.numpy as jnp
import numpy as np
from jax import lax

H = 64
DH = 128
DR = 64
DV = 128
DC = 512
TOK_DEV = 128
SEQ = 1024
DOCS = 8
LWIDTH = 576
KVCOLS = 16384
N_CTX = 8
N_DP = 16


def draw_query(key, part):
    key = jax.random.fold_in(key, 11)
    base_key = jax.random.fold_in(key, 0)
    values = jnp.clip(jax.random.normal(base_key, (N_DP, SEQ, H, DH + DR), jnp.float32), -6.0, 6.0)
    return values.astype(jnp.bfloat16)


def raised(values, stream_key, source, target, blocks, factor):
    owner, partner = [(jnp.arange(values.shape[axis_at]) // (values.shape[axis_at] // blocks)).reshape([-1 if axis == axis_at else 1 for axis in range(values.ndim)]) for axis_at in (source, target)]
    chosen = jax.random.permutation(stream_key, blocks)[partner]
    strong = (owner == chosen) | (owner == (partner + blocks // 2) % blocks)
    return jnp.where(strong, factor * values, values)


def levels(stream_key, extent, pieces, smallest, high):
    def one(axis_at, parts):
        heights = jax.random.uniform(jax.random.fold_in(jax.random.fold_in(stream_key, 6), axis_at), (parts,), jnp.float32, smallest / len(pieces), high / len(pieces))
        return jnp.repeat(jnp.exp(heights), extent[axis_at] // parts).reshape((-1,) + (1,) * (len(extent) - axis_at - 1))

    factor_of = one(*pieces[0])
    for cut in pieces[1:]:
        factor_of = factor_of * one(*cut)
    return factor_of


def split_up(amount, total, reach, slope):
    portions = [(1 << 20) // math.isqrt(grade ** slope) + 1 for grade in range(2, amount + 1)]
    spare, given = total - reach - (amount - 1), [1] * (amount - 1)
    while spare > 0:
        movable = [i for i in range(amount - 1) if given[i] < reach]
        mass, budget = sum([portions[i] for i in movable]), spare
        for i in movable:
            addition = min(reach - given[i], max(1, budget * portions[i] // mass), spare)
            given[i] = given[i] + addition
            spare = spare - addition
    return np.array([reach] + given)


def ragged(stream_key, count, total, reach, lean):
    if count == 2:
        one = jax.random.randint(stream_key, (), max(1, total - reach), min(reach, total - 1) + 1)
        return jnp.stack([one, total - one])
    sizes = jnp.asarray(split_up(count, total, reach, lean), jnp.int32)
    couples = (count - 1) // 2
    source_of, sink = sizes[1:1 + 2 * couples:2], sizes[2:2 + 2 * couples:2]
    room = jnp.minimum(source_of - 1, reach - sink)
    shifted = jax.random.randint(jax.random.fold_in(stream_key, 1), (couples,), 0, 1 << 20) % (room + 1)
    sizes = sizes.at[1:1 + 2 * couples:2].set(source_of - shifted).at[2:2 + 2 * couples:2].set(sink + shifted)
    return sizes[jax.random.permutation(jax.random.fold_in(stream_key, 2), count)]


def gaussian(key, shape, scale, most, cuts=(), held_as=jnp.bfloat16):
    loudness = levels(key, shape, cuts, -0.22, 0.18) if cuts else 1.0
    result = jax.random.normal(key, shape, jnp.float32) * scale * loudness
    return jnp.minimum(jnp.maximum(result, -most), most).astype(held_as)


def noise_with(own_key, dims, deviation, reach, pieces, heavy, kind=jnp.bfloat16):
    values = deviation * jax.random.normal(own_key, dims, jnp.float32)
    if pieces:
        values = values * levels(own_key, dims, pieces, -0.22, 0.18)
    return jnp.clip(raised(values, jax.random.fold_in(own_key, 3), *heavy), -reach, reach).astype(kind)


def setup_inputs(seed: int = 0) -> dict:
    streams_of = jax.random.split(jax.random.key(seed), 6)
    return {
        "query": draw_query(jax.random.fold_in(streams_of[5], 71), 0),
        "latent": gaussian(streams_of[1], (N_DP, SEQ, LWIDTH), 1.0, 6.0, ((0, 16), (1, 8))),
        "doc_lengths": jax.vmap(lambda own: ragged(own, DOCS, SEQ, 2 * TOK_DEV, 2))(jax.random.split(streams_of[2], N_DP)).reshape((N_DP, DOCS)).astype(jnp.int32),
        "w_kv": gaussian(streams_of[3], (KVCOLS, DC), DC ** -0.5, 0.25),
        "grad_out": noise_with(streams_of[4], (N_DP, SEQ, H, DV), 1.0, 6.0, ((0, 16), (1, 8)), (1, 2, 8, 2.0)),
    }


def start_of(lengths, positions):
    ends = jnp.cumsum(lengths).astype(jnp.int32)
    picked = jnp.where(ends[None, :] <= positions[:, None], lengths[None, :], 0)
    return lax.optimization_barrier(jnp.sum(picked, axis=1)).astype(jnp.int32)

def attend(q_block, g_block, k_nope, rope_key, values, allowed, scale):
    f32 = jnp.float32
    q_nope = q_block[..., :DH].astype(f32)
    q_rope = q_block[..., DH:].astype(f32)
    scores = jnp.einsum('qhd,khd->hqk', q_nope, k_nope.astype(f32))
    scores = (scores + jnp.einsum('qhr,kr->hqk', q_rope, rope_key.astype(f32))) * scale
    scores = jnp.where(allowed[None], scores, -jnp.inf)
    top = lax.optimization_barrier(jnp.max(scores, axis=-1, keepdims=True))
    weights = jnp.exp(scores - top)
    probs = weights / lax.optimization_barrier(jnp.sum(weights, axis=-1, keepdims=True))
    probs_bf = probs.astype(jnp.bfloat16)
    gradf = g_block.astype(f32)
    attended = jnp.einsum('hqk,khv->qhv', probs_bf.astype(f32), values.astype(f32)).astype(jnp.bfloat16)
    delta = lax.optimization_barrier(jnp.sum(gradf * attended.astype(f32), axis=-1))
    dprobs = jnp.einsum('qhv,khv->hqk', gradf, values.astype(f32))
    dscores = (probs * (dprobs - delta.T[:, :, None]) * scale).astype(jnp.bfloat16)
    dsf = dscores.astype(f32)
    dq_nope = jnp.einsum('hqk,khd->qhd', dsf, k_nope.astype(f32))
    dq_rope = jnp.einsum('hqk,kr->qhr', dsf, rope_key.astype(f32))
    d_query = jnp.concatenate([dq_nope, dq_rope], axis=-1).astype(jnp.bfloat16)
    dkey = jnp.einsum('hqk,qhd->khd', dsf, q_nope)
    dval = jnp.einsum('hqk,qhv->khv', probs_bf.astype(f32), gradf)
    dkv = jnp.concatenate([dkey, dval], axis=-1).astype(jnp.bfloat16)
    dkv = dkv.reshape(dkv.shape[0], -1)
    drope = jnp.einsum('hqk,qhr->kr', dsf, q_rope)
    return (d_query, dkv, drope)

def one_sequence(query, latent, lengths, w_kv, grad_out):
    rows = TOK_DEV
    scale = 1.0 / math.sqrt(DH + DR)
    kv = jnp.dot(latent[:, :DC], w_kv.T, preferred_element_type=jnp.float32).astype(jnp.bfloat16)
    kv_pad = jnp.concatenate([jnp.zeros((2 * rows, KVCOLS), jnp.bfloat16), kv], axis=0)
    rope_pad = jnp.concatenate([jnp.zeros((2 * rows, DR), jnp.bfloat16), latent[:, DC:]], axis=0)
    starts = start_of(lengths, jnp.arange(SEQ, dtype=jnp.int32))

    def step(carry, block):
        acc_kv, acc_rope = carry
        base = (block * rows).astype(jnp.int32)
        q_block = lax.dynamic_slice_in_dim(query, base, rows, 0)
        g_block = lax.dynamic_slice_in_dim(grad_out, base, rows, 0)
        kv_win = lax.dynamic_slice_in_dim(kv_pad, base, 3 * rows, 0).reshape(3 * rows, H, DH + DV)
        rope_win = lax.dynamic_slice_in_dim(rope_pad, base, 3 * rows, 0)
        qpos = base + jnp.arange(rows, dtype=jnp.int32)
        kpos = base - 2 * rows + jnp.arange(3 * rows, dtype=jnp.int32)
        start_q = lax.dynamic_slice_in_dim(starts, base, rows, 0)
        allowed = (kpos[None, :] >= start_q[:, None]) & (kpos[None, :] <= qpos[:, None])
        d_query, dkv, drope = attend(q_block, g_block, kv_win[..., :DH], rope_win, kv_win[..., DH:], allowed, scale)
        old_kv = lax.dynamic_slice_in_dim(acc_kv, base, 3 * rows, 0)
        acc_kv = lax.dynamic_update_slice_in_dim(acc_kv, old_kv + dkv.astype(jnp.float32), base, 0)
        old_rope = lax.dynamic_slice_in_dim(acc_rope, base, 3 * rows, 0)
        acc_rope = lax.dynamic_update_slice_in_dim(acc_rope, old_rope + drope, base, 0)
        return ((acc_kv, acc_rope), d_query)
    init = (jnp.zeros((SEQ + 2 * rows, KVCOLS), jnp.float32), jnp.zeros((SEQ + 2 * rows, DR), jnp.float32))
    (acc_kv, acc_rope), d_blocks = lax.scan(step, init, jnp.arange(N_CTX, dtype=jnp.int32))
    d_query = d_blocks.reshape(SEQ, H, DH + DR)
    summed = acc_kv[2 * rows:]
    d_lat = jnp.dot(summed, w_kv.astype(jnp.float32), precision=lax.Precision.HIGHEST)
    d_latent = jnp.concatenate([d_lat, acc_rope[2 * rows:]], axis=-1).astype(jnp.bfloat16)
    d_weight = lax.dot_general(summed, latent[:, :DC].astype(jnp.float32), (((0,), (0,)), ((), ())), precision=lax.Precision.HIGHEST)
    return (d_query, d_latent, d_weight)

def reference(query, latent, doc_lengths, w_kv, grad_out):

    def step(total, items):
        q_seq, lat_seq, len_seq, g_seq = items
        d_query, d_latent, d_weight = one_sequence(q_seq, lat_seq, len_seq, w_kv, g_seq)
        return (total + d_weight, (d_query, d_latent))
    total, (d_query, d_latent) = lax.scan(step, jnp.zeros((KVCOLS, DC), jnp.float32), (query, latent, doc_lengths, grad_out))
    return (d_query, d_latent, total)
```

```python
import functools
import math

import jax
import jax.numpy as jnp
from jax import lax
from jax.experimental import pallas as pl
from jax.experimental.pallas import tpu as pltpu
from jax.sharding import Mesh
from jax.sharding import PartitionSpec as P

F32 = jnp.float32
BF16 = jnp.bfloat16
NX, NCORE, NY, NZ = 4, 2, 4, 4
HEADS = 64
NOPE = 128
ROPE = 64
WIDTH = NOPE + ROPE
VDIM = 128
HCOLS = NOPE + VDIM
LAT = 512
ROWS = 128
CHIP = NCORE * ROWS
KEYS = 2 * CHIP
GROUP = 8
PER_STEP = 2
SCALE = 1.0 / math.sqrt(WIDTH)
LOG2E = math.log2(math.e)
NT = (((1,), (1,)), ((), ()))
TN = (((0,), (0,)), ((), ()))


def mm(a, b, dims=(((1,), (0,)), ((), ()))):
    return lax.dot_general(a, b, dims, preferred_element_type=F32)


def heads_kernel(
    info,
    q_own,
    q_got,
    g_own,
    g_got,
    w_ref,
    lat_ref,
    latt_ref,
    rope_ref,
    low_ref,
    dq_keep,
    dq_send,
    dw_a,
    dw_b,
    dlat_ref,
    drope_ref,
    bias_ref,
):
    first_core = info[0] == 0

    @pl.when(pl.program_id(0) == 0)
    def _():
        key = lax.broadcasted_iota(jnp.int32, (KEYS, CHIP), 0)
        row = lax.broadcasted_iota(jnp.int32, (KEYS, CHIP), 1)
        ok = (key >= low_ref[...]) & (key <= row + CHIP)
        bias_ref[...] = jnp.where(ok, 0.0, -1e30)
        dlat_ref[...] = jnp.zeros_like(dlat_ref)
        drope_ref[...] = jnp.zeros_like(drope_ref)

    lat = lat_ref[...]
    latt = latt_ref[...]
    rope = rope_ref[...]
    dkvs = []
    for i in range(PER_STEP):
        qo, qr, go, gr = q_own[i], q_got[i], g_own[i], g_got[i]
        q = jnp.concatenate([jnp.where(first_core, qo, qr), jnp.where(first_core, qr, qo)], axis=0)
        g = jnp.concatenate([jnp.where(first_core, go, gr), jnp.where(first_core, gr, go)], axis=0)
        w = w_ref[i * HCOLS : (i + 1) * HCOLS]
        kv = mm(lat, w, NT).astype(BF16)
        v = kv[:, NOPE:]
        k = jnp.concatenate([kv[:, :NOPE], rope], axis=1)
        s = mm(k, q, NT) * (SCALE * LOG2E) + bias_ref[...]
        e = jnp.exp2(s - jnp.max(s, axis=0, keepdims=True))
        p = e * (1.0 / jnp.sum(e, axis=0, keepdims=True))
        dp = mm(v, g, NT)
        delta = jnp.sum(p * dp, axis=0, keepdims=True)
        ds = (p * ((dp - delta) * SCALE)).astype(BF16)
        dq = mm(ds, k, TN).astype(BF16)
        dq_keep[i] = jnp.where(first_core, dq[:ROWS], dq[ROWS:])
        dq_send[i] = jnp.where(first_core, dq[ROWS:], dq[:ROWS])
        dk = mm(ds, q)
        dv = mm(p.astype(BF16), g)
        drope_ref[...] += dk[:, NOPE:]
        dkv = jnp.concatenate([dk[:, :NOPE], dv], axis=1).astype(BF16)
        dkvs.append(dkv)
        dw = mm(latt, dkv).astype(BF16)
        for half in range(2):
            part = dw[:, half * 128 : (half + 1) * 128]
            dw_a[0, 2 * i + half] = part[: LAT // 2]
            dw_b[2 * i + half, 0] = part[LAT // 2 :]
    dlat_ref[...] += mm(jnp.concatenate(dkvs, axis=1), w_ref[...])


def head_group(group, info, q_own, q_got, g_own, g_got, w_kv, lat, latt, rope, low):
    steps = GROUP // PER_STEP
    per_head = lambda i, info: (group * steps + i, 0, 0)
    whole = lambda i, info: (0, 0)
    w_rows = lambda i, info: ((2 * group + info[0]) * steps + i, 0)
    out_head = lambda i, info: (i, 0, 0)
    n_dw = 2 * PER_STEP
    grid_spec = pltpu.PrefetchScalarGridSpec(
        num_scalar_prefetch=1,
        grid=(steps,),
        in_specs=[
            pl.BlockSpec((PER_STEP, ROWS, WIDTH), per_head),
            pl.BlockSpec((PER_STEP, ROWS, WIDTH), per_head),
            pl.BlockSpec((PER_STEP, ROWS, VDIM), per_head),
            pl.BlockSpec((PER_STEP, ROWS, VDIM), per_head),
            pl.BlockSpec((PER_STEP * HCOLS, LAT), w_rows),
            pl.BlockSpec((KEYS, LAT), whole),
            pl.BlockSpec((LAT, KEYS), whole),
            pl.BlockSpec((KEYS, ROPE), whole),
            pl.BlockSpec((1, CHIP), whole),
        ],
        out_specs=[
            pl.BlockSpec((PER_STEP, ROWS, WIDTH), out_head),
            pl.BlockSpec((PER_STEP, ROWS, WIDTH), out_head),
            pl.BlockSpec((1, n_dw, LAT // 2, 128), lambda i, info: (i, 0, 0, 0)),
            pl.BlockSpec((n_dw, 1, LAT // 2, 128), lambda i, info: (0, i, 0, 0)),
            pl.BlockSpec((KEYS, LAT), whole),
            pl.BlockSpec((KEYS, ROPE), whole),
        ],
        scratch_shapes=[pltpu.VMEM((KEYS, CHIP), F32)],
    )
    flops = 2 * GROUP * (3 * KEYS * LAT * HCOLS + KEYS * CHIP * (3 * WIDTH + 2 * VDIM))
    return pl.pallas_call(
        heads_kernel,
        grid_spec=grid_spec,
        out_shape=[
            jax.ShapeDtypeStruct((GROUP, ROWS, WIDTH), BF16),
            jax.ShapeDtypeStruct((GROUP, ROWS, WIDTH), BF16),
            jax.ShapeDtypeStruct((NY, NZ, LAT // 2, 128), BF16),
            jax.ShapeDtypeStruct((NZ, NY, LAT // 2, 128), BF16),
            jax.ShapeDtypeStruct((KEYS, LAT), F32),
            jax.ShapeDtypeStruct((KEYS, ROPE), F32),
        ],
        compiler_params=pltpu.CompilerParams(
            dimension_semantics=("arbitrary",), vmem_limit_bytes=48 * 1024 * 1024
        ),
        cost_estimate=pl.CostEstimate(
            flops=flops, bytes_accessed=12 * 1024 * 1024, transcendentals=GROUP * KEYS * CHIP
        ),
        name="heads",
    )(info, q_own, q_got, g_own, g_got, w_kv, lat, latt, rope, low)


def start_of(lengths, positions):
    ends = jnp.cumsum(lengths)
    picked = jnp.where(ends[None, :] <= positions[:, None], lengths[None, :], 0)
    return jnp.sum(picked, axis=1)


def ring(distance):
    return [(i, (i + distance) % 4) for i in range(4)]


def pick(blocks, index):
    return lax.dynamic_index_in_dim(blocks, index, 0, keepdims=False)


def exchange(blocks, axis, me):
    got = [pick(blocks, me)]
    for distance in (1, 3, 2):
        sent = pick(blocks, lax.rem(me + distance, 4))
        got.append(lax.ppermute(sent, axis, ring(distance)))
    return got


def total(parts):
    return functools.reduce(jnp.add, [part.astype(F32) for part in parts])


def per_device(query, latent, doc_lengths, w_kv, grad_out):
    x, core = lax.axis_index("x"), lax.axis_index("core")
    y, z = lax.axis_index("y"), lax.axis_index("z")
    first_core = core == 0
    swap = [(0, 1), (1, 0)]

    own = latent[0]
    both = ("x", "core")
    mate = lax.ppermute(own, "core", swap)
    prev_same = lax.ppermute(own, both, [(2 * i + c, 2 * i + 2 + c) for i in range(3) for c in range(2)])
    prev_mate = lax.ppermute(
        own, both, [(2 * i + c, 2 * i + 2 + 1 - c) for i in range(3) for c in range(2)]
    )

    def ordered(mine, other):
        return [jnp.where(first_core, mine, other), jnp.where(first_core, other, mine)]

    def split(block):
        block = block.reshape(ROWS, NX, NCORE, GROUP, block.shape[-1])
        return [
            lax.dynamic_index_in_dim(block, which, 2, keepdims=False)
            .reshape(ROWS, NX * GROUP, block.shape[-1])
            .transpose(1, 0, 2)
            for which in (core, 1 - core)
        ]

    q_own, q_out = split(query[0])
    g_own, g_out = split(grad_out[0])
    q_got = lax.ppermute(q_out, "core", swap)
    g_got = lax.ppermute(g_out, "core", swap)

    window = jnp.concatenate(ordered(prev_same, prev_mate) + ordered(own, mate), axis=0)
    lat = window[:, :LAT]
    rope = window[:, LAT:]
    latt = lat.T
    base = x * CHIP
    starts = start_of(doc_lengths[0], base + jnp.arange(CHIP, dtype=jnp.int32))
    low = (starts - (base - CHIP)).astype(jnp.int32).reshape(1, CHIP)
    info = core.astype(jnp.int32).reshape(1)

    keeps, sends, dlats, dropes = [], [], [], []
    a_mid, b_mid = [], []
    for group in range(NX):
        keep, send, dw_a, dw_b, dlat, drope = head_group(
            group, info, q_own, q_got, g_own, g_got, w_kv, lat, latt, rope, low
        )
        keeps.append(keep)
        sends.append(send)
        dlats.append(dlat)
        dropes.append(drope)
        a_mid.append(total(exchange(dw_a, "y", y)).astype(BF16))
        b_mid.append(total(exchange(dw_b, "z", z)).astype(BF16))

    def second(lo, hi):
        a = jnp.stack(a_mid[lo:hi], axis=1)
        b = jnp.stack(b_mid[lo:hi], axis=1)
        a = total(exchange(a, "z", z)).astype(BF16)
        b = total(exchange(b, "y", y)).astype(BF16)
        return jnp.concatenate([a, b], axis=1)

    last = jnp.concatenate([second(0, 3), second(3, 4)], axis=0)
    d_weight = total(exchange(last, "x", x)).T

    terms = jnp.concatenate([total(dlats), total(dropes)], axis=-1)
    blocks = terms.reshape(4, ROWS, LAT + ROPE)
    mine = pick(blocks, 2 + core)
    from_mate = lax.ppermute(pick(blocks, 3 - core).astype(BF16), "core", swap)
    from_next = lax.ppermute(
        pick(blocks, core).astype(BF16),
        both,
        [(2 * i + 2 + c, 2 * i + c) for i in range(3) for c in range(2)],
    )
    from_next_mate = lax.ppermute(
        pick(blocks, 1 - core).astype(BF16),
        both,
        [(2 * i + 2 + c, 2 * i + 1 - c) for i in range(3) for c in range(2)],
    )
    d_latent = total([mine, from_mate, from_next, from_next_mate]).astype(BF16)

    dq_mine = jnp.stack(keeps, axis=0)
    dq_got = lax.ppermute(jnp.stack(sends, axis=0), "core", swap)
    d_query = jnp.stack(ordered(dq_mine, dq_got), axis=1).reshape(HEADS, ROWS, WIDTH)
    return (d_query.transpose(1, 0, 2)[None], d_latent[None], d_weight)


def solution(mesh):
    fine = Mesh(mesh.devices.reshape(NX, NCORE, NY, NZ), ("x", "core", "y", "z"))
    dp, ctx = ("y", "z"), ("x", "core")
    in_specs = (P(dp, ctx, None, None), P(dp, ctx, None), P(dp, None), P(), P(dp, ctx, None, None))
    out_specs = (P(dp, ctx, None, None), P(dp, ctx, None), P(("x", "core", "y", "z"), None))
    return jax.shard_map(
        per_device, mesh=fine, in_specs=in_specs, out_specs=out_specs, check_vma=False
    )
```

```python
import functools
import math

import jax
import jax.numpy as jnp
from jax import lax
from jax.experimental import pallas as pl
from jax.experimental.pallas import tpu as pltpu
from jax.sharding import Mesh
from jax.sharding import PartitionSpec as P

F32 = jnp.float32
BF16 = jnp.bfloat16
NX, NCORE, NY, NZ = 4, 2, 4, 4
HEADS = 64
NOPE = 128
ROPE = 64
WIDTH = NOPE + ROPE
VDIM = 128
HCOLS = NOPE + VDIM
LAT = 512
ROWS = 128
CHIP = NCORE * ROWS
KEYS = 2 * CHIP
GROUP = 8
PER_STEP = 4
SCALE = 1.0 / math.sqrt(WIDTH)
LOG2E = math.log2(math.e)
NT = (((1,), (1,)), ((), ()))
TN = (((0,), (0,)), ((), ()))


def mm(a, b, dims=(((1,), (0,)), ((), ()))):
    return lax.dot_general(a, b, dims, preferred_element_type=F32)


def main_kernel(leading, *refs):
    info, q_own, q_got, g_own, g_got, w_ref, lat_ref, latt_ref, rope_ref, low_ref = refs[:10]
    dq_ref, send_ref, dw_ref, dlat_ref, drope_ref, bias_ref = refs[-6:]
    first_core = info[0] == 0

    @pl.when(pl.program_id(0) == 0)
    def _():
        key = lax.broadcasted_iota(jnp.int32, (KEYS, CHIP), 0)
        row = lax.broadcasted_iota(jnp.int32, (KEYS, CHIP), 1)
        ok = (key >= low_ref[...]) & (key <= row + CHIP)
        bias_ref[...] = jnp.where(ok, 0.0, -1e30)
        if leading:
            dlat_ref[...] = jnp.zeros_like(dlat_ref)
            drope_ref[...] = jnp.zeros_like(drope_ref)
        else:
            dlat_ref[...] = refs[10][...]
            drope_ref[...] = refs[11][...]

    rope = rope_ref[...]
    kv_all = mm(lat_ref[...], w_ref[...], NT).astype(BF16)
    dkvs, dropes = [], []
    for i in range(PER_STEP):
        qo, qr, go, gr = q_own[i], q_got[i], g_own[i], g_got[i]
        q = jnp.concatenate([jnp.where(first_core, qo, qr), jnp.where(first_core, qr, qo)], axis=1)
        g = jnp.concatenate([jnp.where(first_core, go, gr), jnp.where(first_core, gr, go)], axis=0)
        col = i * HCOLS
        k = jnp.concatenate([kv_all[:, col : col + NOPE], rope], axis=1)
        v = kv_all[:, col + NOPE : col + HCOLS]
        s = mm(k, q) * (SCALE * LOG2E) + bias_ref[...]
        e = jnp.exp2(s - jnp.max(s, axis=0, keepdims=True))
        r = 1.0 / jnp.sum(e, axis=0, keepdims=True)
        dp = mm(v, g, NT)
        delta = jnp.sum(e * dp, axis=0, keepdims=True) * r
        rs = r * SCALE
        ds = (e * (dp * rs - delta * rs)).astype(BF16)
        dq = mm(k, ds, TN).astype(BF16)
        dq_ref[i] = jnp.where(first_core, dq[:, :ROWS], dq[:, ROWS:])
        send_ref[i] = jnp.where(first_core, dq[:, ROWS:], dq[:, :ROWS])
        dk = mm(ds, q, NT)
        dv = mm((e * r).astype(BF16), g)
        dropes.append(dk[:, NOPE:])
        dkvs.append(jnp.concatenate([dk[:, :NOPE], dv], axis=1).astype(BF16))
    drope_ref[...] += functools.reduce(jnp.add, dropes)
    dkv = jnp.concatenate(dkvs, axis=1)
    dw = mm(latt_ref[...], dkv).astype(BF16)
    for j in range(2 * PER_STEP):
        part = dw[:, j * 128 : (j + 1) * 128]
        dw_ref[j // NZ, j % NZ] = part
    dlat_ref[...] += mm(dkv, w_ref[...])


def main_group(info, q_full, q_got, g_full, g_got, w_kv, lat, latt, rope, low, state):
    steps = GROUP // PER_STEP
    half = lambda i, info: (info[1] * steps + i, 0, 0)
    full = lambda i, info: ((2 * info[1] + info[0]) * steps + i, 0, 0)
    whole = lambda i, info: (0, 0)
    w_rows = lambda i, info: ((2 * info[1] + info[0]) * steps + i, 0)
    ys = 2 * PER_STEP // NZ
    in_specs = [
        pl.BlockSpec((PER_STEP, WIDTH, ROWS), full),
        pl.BlockSpec((PER_STEP, WIDTH, ROWS), half),
        pl.BlockSpec((PER_STEP, ROWS, VDIM), full),
        pl.BlockSpec((PER_STEP, ROWS, VDIM), half),
        pl.BlockSpec((PER_STEP * HCOLS, LAT), w_rows),
        pl.BlockSpec((KEYS, LAT), whole),
        pl.BlockSpec((LAT, KEYS), whole),
        pl.BlockSpec((KEYS, ROPE), whole),
        pl.BlockSpec((1, CHIP), whole),
    ]
    aliases = {}
    if state:
        in_specs += [
            pl.BlockSpec((KEYS, LAT), whole),
            pl.BlockSpec((KEYS, ROPE), whole),
            pl.BlockSpec(memory_space=pl.ANY),
            pl.BlockSpec(memory_space=pl.ANY),
        ]
        aliases = {12: 0, 13: 1}
    grid_spec = pltpu.PrefetchScalarGridSpec(
        num_scalar_prefetch=1,
        grid=(steps,),
        in_specs=in_specs,
        out_specs=[
            pl.BlockSpec((PER_STEP, WIDTH, ROWS), full),
            pl.BlockSpec((PER_STEP, WIDTH, ROWS), half),
            pl.BlockSpec((ys, NZ, LAT, 128), lambda i, info: (i, 0, 0, 0)),
            pl.BlockSpec((KEYS, LAT), whole),
            pl.BlockSpec((KEYS, ROPE), whole),
        ],
        scratch_shapes=[pltpu.VMEM((KEYS, CHIP), F32)],
    )
    flops = 2 * GROUP * KEYS * CHIP
    return pl.pallas_call(
        functools.partial(main_kernel, not state),
        grid_spec=grid_spec,
        out_shape=[
            pltpu.HBM((HEADS, WIDTH, ROWS), BF16),
            pltpu.HBM((HEADS // 2, WIDTH, ROWS), BF16),
            pltpu.HBM((4, 4, LAT, 128), BF16),
            pltpu.HBM((KEYS, LAT), F32),
            pltpu.HBM((KEYS, ROPE), F32),
        ],
        input_output_aliases=aliases,
        compiler_params=pltpu.CompilerParams(
            dimension_semantics=("arbitrary",), vmem_limit_bytes=48 * 1024 * 1024
        ),
        cost_estimate=pl.CostEstimate(
            flops=flops, bytes_accessed=10 * 1024 * 1024, transcendentals=0
        ),
        name="main_group",
    )(info, q_full, q_got, g_full, g_got, w_kv, lat, latt, rope, low, *state)


def window_kernel(info, own, mate, prev_same, prev_mate, lat_ref, latt_ref, rope_ref):
    first_core = info[0] == 0

    def pair(mine, other):
        return [jnp.where(first_core, mine, other), jnp.where(first_core, other, mine)]

    window = jnp.concatenate(
        pair(prev_same[...], prev_mate[...]) + pair(own[...], mate[...]), axis=1
    )
    latt_ref[...] = window[:LAT]
    lat_ref[...] = window[:LAT].T
    rope_ref[...] = window[LAT:].T


def window_of(info, pieces):
    return pl.pallas_call(
        window_kernel,
        in_specs=[pl.BlockSpec(memory_space=pltpu.SMEM)]
        + [pl.BlockSpec(memory_space=pltpu.VMEM)] * 4,
        out_shape=[
            jax.ShapeDtypeStruct((KEYS, LAT), BF16),
            jax.ShapeDtypeStruct((LAT, KEYS), BF16),
            jax.ShapeDtypeStruct((KEYS, ROPE), BF16),
        ],
        compiler_params=pltpu.CompilerParams(vmem_limit_bytes=32 * 1024 * 1024),
        name="window",
    )(info, *pieces)


def place_kernel(info, got_ref, held_ref, out_ref):
    out_ref[...] = got_ref[...]


def place(info, got, held):
    block = (GROUP, WIDTH, ROWS)
    grid_spec = pltpu.PrefetchScalarGridSpec(
        num_scalar_prefetch=1,
        grid=(NX,),
        in_specs=[
            pl.BlockSpec(block, lambda i, info: (i, 0, 0)),
            pl.BlockSpec(memory_space=pl.ANY),
        ],
        out_specs=pl.BlockSpec(block, lambda i, info: (2 * i + 1 - info[0], 0, 0)),
    )
    return pl.pallas_call(
        place_kernel,
        grid_spec=grid_spec,
        out_shape=pltpu.HBM((HEADS, WIDTH, ROWS), BF16),
        input_output_aliases={2: 0},
        compiler_params=pltpu.CompilerParams(dimension_semantics=("arbitrary",)),
        cost_estimate=pl.CostEstimate(flops=0, bytes_accessed=4 * 1024 * 1024, transcendentals=0),
        name="place",
    )(info, got, held)


def start_of(lengths, positions):
    ends = jnp.cumsum(lengths)
    picked = jnp.where(ends[None, :] <= positions[:, None], lengths[None, :], 0)
    return jnp.sum(picked, axis=1)


def ring(distance):
    return [(i, (i + distance) % 4) for i in range(4)]


def pick(blocks, index):
    return lax.dynamic_index_in_dim(blocks, index, 0, keepdims=False)


def exchange(blocks, axis, me):
    got = [pick(blocks, me)]
    for distance in (1, 3, 2):
        sent = pick(blocks, lax.rem(me + distance, 4))
        got.append(lax.ppermute(sent, axis, ring(distance)))
    return got


def total(parts):
    return functools.reduce(jnp.add, [part.astype(F32) for part in parts])


def all_to_all(blocks, axis):
    return lax.all_to_all(blocks, axis, 0, 0, tiled=True)


def summed(parts):
    return jnp.sum(parts.astype(F32), axis=0).astype(BF16)


def per_device(query, latent, doc_lengths, w_kv, grad_out):
    x, core = lax.axis_index("x"), lax.axis_index("core")
    y, z = lax.axis_index("y"), lax.axis_index("z")
    swap = [(0, 1), (1, 0)]
    both = ("x", "core")
    tie = lax.optimization_barrier

    def other_half(full):
        parts = full.reshape(NX, NCORE, GROUP, full.shape[1], full.shape[2])
        chosen = lax.dynamic_index_in_dim(parts, 1 - core, 1, keepdims=False)
        return chosen.reshape(HEADS // 2, full.shape[1], full.shape[2])

    own = latent[0].T
    mate = lax.ppermute(own, "core", swap)
    prev_same = lax.ppermute(own, both, [(2 * i + c, 2 * i + 2 + c) for i in range(3) for c in range(2)])
    prev_mate = lax.ppermute(
        own, both, [(2 * i + c, 2 * i + 2 + 1 - c) for i in range(3) for c in range(2)]
    )
    q_full = query[0].transpose(1, 2, 0)
    q_got = lax.ppermute(other_half(q_full), "core", swap)
    g_full = tie(grad_out[0].transpose(1, 0, 2))
    g_got = lax.ppermute(other_half(g_full), "core", swap)

    core_info = core.astype(jnp.int32).reshape(1)
    lat, latt, rope = window_of(core_info, (own, mate, prev_same, prev_mate))
    base = x * CHIP
    starts = start_of(doc_lengths[0], base + jnp.arange(CHIP, dtype=jnp.int32))
    low = (starts - (base - CHIP)).astype(jnp.int32).reshape(1, CHIP)

    def main(ahead, state):
        group = lax.rem(x + ahead, NX)
        info = jnp.stack([core, group]).astype(jnp.int32)
        dq, send, dw, dlat, drope = main_group(
            info, q_full, q_got, g_full, g_got, w_kv, lat, latt, rope, low, state
        )
        return dw, (dlat, drope, dq, send)

    dw, state = main(1, ())
    from_left = lax.ppermute(dw, "x", ring(1))
    dw, state = main(3, state)
    from_right = lax.ppermute(dw, "x", ring(3))
    dw, state = main(2, state)
    across = all_to_all(dw, "y")
    dw, state = main(0, state)
    dlat, drope, dq, send = state

    across = summed(across)
    mine = total([dw, from_left, from_right]).astype(BF16)
    part_a = all_to_all(mine[:, :, : LAT // 2], "y")
    rows_b = NY * LAT // 2
    part_b = jnp.swapaxes(mine[:, :, LAT // 2 :], 0, 1).reshape(NZ, rows_b, 128)
    part_b = total(exchange(jnp.concatenate([part_b, across], axis=1), "z", z))
    across = lax.ppermute(part_b[rows_b:].astype(BF16), "x", ring(2))
    part_b = part_b[:rows_b].astype(BF16).reshape(NY, LAT // 2, 128)
    part_b = all_to_all(part_b, "y")
    part_a = total(exchange(summed(part_a), "z", z))
    part_b = jnp.sum(part_b.astype(F32), axis=0)
    d_weight = (jnp.concatenate([part_a, part_b], axis=0) + across.astype(F32)).T

    terms = jnp.concatenate([dlat, drope], axis=-1)
    blocks = terms.reshape(4, ROWS, LAT + ROPE)
    mine = pick(blocks, 2 + core)
    from_mate = lax.ppermute(pick(blocks, 3 - core).astype(BF16), "core", swap)
    from_next = lax.ppermute(
        pick(blocks, core).astype(BF16),
        both,
        [(2 * i + 2 + c, 2 * i + c) for i in range(3) for c in range(2)],
    )
    from_next_mate = lax.ppermute(
        pick(blocks, 1 - core).astype(BF16),
        both,
        [(2 * i + 2 + c, 2 * i + 1 - c) for i in range(3) for c in range(2)],
    )
    d_latent = total([mine, from_mate, from_next, from_next_mate]).astype(BF16)

    got = lax.ppermute(send, "core", swap)
    d_query = place(core_info, got, dq)
    return (d_query.transpose(2, 0, 1)[None], d_latent[None], d_weight)


def solution(mesh):
    fine = Mesh(mesh.devices.reshape(NX, NCORE, NY, NZ), ("x", "core", "y", "z"))
    dp, ctx = ("y", "z"), ("x", "core")
    in_specs = (P(dp, ctx, None, None), P(dp, ctx, None), P(dp, None), P(), P(dp, ctx, None, None))
    out_specs = (P(dp, ctx, None, None), P(dp, ctx, None), P(("x", "core", "y", "z"), None))
    return jax.shard_map(
        per_device, mesh=fine, in_specs=in_specs, out_specs=out_specs, check_vma=False
    )
```

```python
import functools
import math

import jax
import jax.numpy as jnp
from jax import lax
from jax.experimental import pallas as pl
from jax.experimental.pallas import tpu as pltpu
from jax.sharding import Mesh
from jax.sharding import PartitionSpec as P

F32 = jnp.float32
BF16 = jnp.bfloat16
NX, NCORE, NY, NZ = 4, 2, 4, 4
HEADS = 64
NOPE = 128
ROPE = 64
WIDTH = NOPE + ROPE
VDIM = 128
HCOLS = NOPE + VDIM
LAT = 512
ROWS = 128
CHIP = NCORE * ROWS
KEYS = 2 * CHIP
GROUP = 8
PER_STEP = 4
STEPS = GROUP // PER_STEP
SCALE = 1.0 / math.sqrt(WIDTH)
LOG2E = math.log2(math.e)
NT = (((1,), (1,)), ((), ()))
TN = (((0,), (0,)), ((), ()))


def mm(a, b, dims=(((1,), (0,)), ((), ()))):
    return lax.dot_general(a, b, dims, preferred_element_type=F32)


def main_kernel(groups, info, *refs):
    q_own, q_got, g_own, g_got, w_ref, lat_ref, latt_ref, rope_ref, low_ref = refs[:9]
    dlat_ref, drope_ref, bias_ref = refs[-3:]
    dw_refs = refs[-3 - groups : -3]
    dq_ref, send_ref = refs[-5 - groups : -3 - groups]
    first_core = info[0] == 0
    step = pl.program_id(0)

    @pl.when(step == 0)
    def _():
        key = lax.broadcasted_iota(jnp.int32, (KEYS, CHIP), 0)
        row = lax.broadcasted_iota(jnp.int32, (KEYS, CHIP), 1)
        ok = (key >= low_ref[...]) & (key <= row + CHIP)
        bias_ref[...] = jnp.where(ok, 0.0, -1e30)
        dlat_ref[...] = jnp.zeros_like(dlat_ref)
        drope_ref[...] = jnp.zeros_like(drope_ref)

    rope = rope_ref[...]
    kv_all = mm(lat_ref[...], w_ref[...], NT).astype(BF16)
    dkvs, dropes = [], []
    for i in range(PER_STEP):
        qo, qr, go, gr = q_own[i], q_got[i], g_own[i], g_got[i]
        q = jnp.concatenate([jnp.where(first_core, qo, qr), jnp.where(first_core, qr, qo)], axis=1)
        g = jnp.concatenate([jnp.where(first_core, go, gr), jnp.where(first_core, gr, go)], axis=0)
        col = i * HCOLS
        k = jnp.concatenate([kv_all[:, col : col + NOPE], rope], axis=1)
        v = kv_all[:, col + NOPE : col + HCOLS]
        s = mm(k, q) * (SCALE * LOG2E) + bias_ref[...]
        e = jnp.exp2(s - jnp.max(s, axis=0, keepdims=True))
        r = 1.0 / jnp.sum(e, axis=0, keepdims=True)
        dp = mm(v, g, NT)
        delta = jnp.sum(e * dp, axis=0, keepdims=True) * r
        rs = r * SCALE
        ds = (e * (dp * rs - delta * rs)).astype(BF16)
        dq = mm(k, ds, TN).astype(BF16)
        dq_ref[i] = jnp.where(first_core, dq[:, :ROWS], dq[:, ROWS:])
        send_ref[i] = jnp.where(first_core, dq[:, ROWS:], dq[:, :ROWS])
        dk = mm(ds, q, NT)
        dv = mm((e * r).astype(BF16), g)
        dropes.append(dk[:, NOPE:])
        dkvs.append(jnp.concatenate([dk[:, :NOPE], dv], axis=1).astype(BF16))
    drope_ref[...] += functools.reduce(jnp.add, dropes)
    dkv = jnp.concatenate(dkvs, axis=1)
    dw = mm(latt_ref[...], dkv).astype(BF16)
    for group, dw_ref in enumerate(dw_refs):

        @pl.when(step // STEPS == group)
        def _():
            for j in range(2 * PER_STEP):
                dw_ref[j // NZ, j % NZ] = dw[:, j * 128 : (j + 1) * 128]

    dlat_ref[...] += mm(dkv, w_ref[...])


def main_groups(groups, info, q_full, q_got, g_full, g_got, w_kv, lat, latt, rope, low, held):
    group_of = lambda i, info: info[1 + i // STEPS]
    half = lambda i, info: (group_of(i, info) * STEPS + i % STEPS, 0, 0)
    full = lambda i, info: ((2 * group_of(i, info) + info[0]) * STEPS + i % STEPS, 0, 0)
    w_rows = lambda i, info: ((2 * group_of(i, info) + info[0]) * STEPS + i % STEPS, 0)
    whole = lambda i, info: (0, 0)
    ys = 2 * PER_STEP // NZ

    def dw_spec(group):
        def index(i, info):
            return (jnp.clip(i - group * STEPS, 0, STEPS - 1), 0, 0, 0)

        return pl.BlockSpec((ys, NZ, LAT, 128), index)

    in_specs = [
        pl.BlockSpec((PER_STEP, WIDTH, ROWS), full),
        pl.BlockSpec((PER_STEP, WIDTH, ROWS), full),
        pl.BlockSpec((PER_STEP, ROWS, VDIM), full),
        pl.BlockSpec((PER_STEP, ROWS, VDIM), half),
        pl.BlockSpec((PER_STEP * HCOLS, LAT), w_rows),
        pl.BlockSpec((KEYS, LAT), whole),
        pl.BlockSpec((LAT, KEYS), whole),
        pl.BlockSpec((KEYS, ROPE), whole),
        pl.BlockSpec((1, CHIP), whole),
    ]
    aliases = {}
    if held:
        in_specs += [pl.BlockSpec(memory_space=pl.ANY)] * 2
        aliases = {10: 0, 11: 1}
    grid_spec = pltpu.PrefetchScalarGridSpec(
        num_scalar_prefetch=1,
        grid=(groups * STEPS,),
        in_specs=in_specs,
        out_specs=[
            pl.BlockSpec((PER_STEP, WIDTH, ROWS), full),
            pl.BlockSpec((PER_STEP, WIDTH, ROWS), half),
        ]
        + [dw_spec(group) for group in range(groups)]
        + [pl.BlockSpec((KEYS, LAT), whole), pl.BlockSpec((KEYS, ROPE), whole)],
        scratch_shapes=[pltpu.VMEM((KEYS, CHIP), F32)],
    )
    outs = pl.pallas_call(
        functools.partial(main_kernel, groups),
        grid_spec=grid_spec,
        out_shape=[
            pltpu.HBM((HEADS, WIDTH, ROWS), BF16),
            pltpu.HBM((HEADS // 2, WIDTH, ROWS), BF16),
        ]
        + [pltpu.HBM((NY, NZ, LAT, 128), BF16)] * groups
        + [pltpu.HBM((KEYS, LAT), F32), pltpu.HBM((KEYS, ROPE), F32)],
        input_output_aliases=aliases,
        compiler_params=pltpu.CompilerParams(
            dimension_semantics=("arbitrary",), vmem_limit_bytes=48 * 1024 * 1024
        ),
        cost_estimate=pl.CostEstimate(
            flops=0, bytes_accessed=0, transcendentals=0
        ),
        name="main_groups",
    )(info, q_full, q_got, g_full, g_got, w_kv, lat, latt, rope, low, *held)
    return tuple(outs[:2]), outs[2 : 2 + groups], (outs[-2], outs[-1])


def fold_kernel(*refs):
    parts, (wide_ref, narrow_ref) = refs[:-2], refs[-2:]
    dlat = functools.reduce(jnp.add, [ref[...] for ref in parts[0::2]])
    drope = functools.reduce(jnp.add, [ref[...] for ref in parts[1::2]])
    block = jnp.concatenate([dlat.T, drope.T], axis=0)
    wide_ref[0] = block
    narrow_ref[0] = block.astype(BF16)


def fold(parts):
    width = LAT + ROPE
    rows = lambda j: (j, 0)
    out = pl.BlockSpec((1, width, ROWS), lambda j: (j, 0, 0))
    return pl.pallas_call(
        fold_kernel,
        grid=(KEYS // ROWS,),
        in_specs=[pl.BlockSpec((ROWS, LAT), rows), pl.BlockSpec((ROWS, ROPE), rows)] * len(parts),
        out_specs=[out, out],
        out_shape=[
            jax.ShapeDtypeStruct((4, width, ROWS), F32),
            jax.ShapeDtypeStruct((4, width, ROWS), BF16),
        ],
        compiler_params=pltpu.CompilerParams(dimension_semantics=("arbitrary",)),
        cost_estimate=pl.CostEstimate(flops=0, bytes_accessed=0, transcendentals=0),
        name="fold",
    )(*[array for pair in parts for array in pair])


def window_kernel(info, own, mate, prev_same, prev_mate, lat_ref, latt_ref, rope_ref):
    first_core = info[0] == 0

    def pair(mine, other):
        return [jnp.where(first_core, mine, other), jnp.where(first_core, other, mine)]

    window = jnp.concatenate(
        pair(prev_same[...], prev_mate[...]) + pair(own[...], mate[...]), axis=1
    )
    latt_ref[...] = window[:LAT]
    lat_ref[...] = window[:LAT].T
    rope_ref[...] = window[LAT:].T


def window_of(info, pieces):
    return pl.pallas_call(
        window_kernel,
        in_specs=[pl.BlockSpec(memory_space=pltpu.SMEM)]
        + [pl.BlockSpec(memory_space=pltpu.VMEM)] * 4,
        out_shape=[
            jax.ShapeDtypeStruct((KEYS, LAT), BF16),
            jax.ShapeDtypeStruct((LAT, KEYS), BF16),
            jax.ShapeDtypeStruct((KEYS, ROPE), BF16),
        ],
        compiler_params=pltpu.CompilerParams(vmem_limit_bytes=32 * 1024 * 1024),
        name="window",
    )(info, *pieces)


def place_kernel(info, got_ref, held_ref, out_ref):
    out_ref[...] = got_ref[...]


def place(info, got, held):
    block = (GROUP, WIDTH, ROWS)
    grid_spec = pltpu.PrefetchScalarGridSpec(
        num_scalar_prefetch=1,
        grid=(NX,),
        in_specs=[
            pl.BlockSpec(block, lambda i, info: (i, 0, 0)),
            pl.BlockSpec(memory_space=pl.ANY),
        ],
        out_specs=pl.BlockSpec(block, lambda i, info: (2 * i + 1 - info[0], 0, 0)),
    )
    return pl.pallas_call(
        place_kernel,
        grid_spec=grid_spec,
        out_shape=pltpu.HBM((HEADS, WIDTH, ROWS), BF16),
        input_output_aliases={2: 0},
        compiler_params=pltpu.CompilerParams(dimension_semantics=("arbitrary",)),
        cost_estimate=pl.CostEstimate(flops=0, bytes_accessed=0, transcendentals=0),
        name="place",
    )(info, got, held)


def start_of(lengths, positions):
    ends = jnp.cumsum(lengths)
    picked = jnp.where(ends[None, :] <= positions[:, None], lengths[None, :], 0)
    return jnp.sum(picked, axis=1)


def ring(distance):
    return [(i, (i + distance) % 4) for i in range(4)]


def pick(blocks, index):
    return lax.dynamic_index_in_dim(blocks, index, 0, keepdims=False)


def exchange(blocks, axis, me):
    got = [pick(blocks, me)]
    for distance in (1, 3, 2):
        sent = pick(blocks, lax.rem(me + distance, 4))
        got.append(lax.ppermute(sent, axis, ring(distance)))
    return got


def total(parts):
    return functools.reduce(jnp.add, [part.astype(F32) for part in parts])


def all_to_all(blocks, axis):
    return lax.all_to_all(blocks, axis, 0, 0, tiled=True)


def summed(parts):
    return jnp.sum(parts.astype(F32), axis=0).astype(BF16)


def per_device(query, latent, doc_lengths, w_kv, grad_out):
    x, core = lax.axis_index("x"), lax.axis_index("core")
    y, z = lax.axis_index("y"), lax.axis_index("z")
    swap = [(0, 1), (1, 0)]
    tie = lax.optimization_barrier

    def other_half(full):
        parts = full.reshape(NX, NCORE, GROUP, full.shape[1], full.shape[2])
        chosen = lax.dynamic_index_in_dim(parts, 1 - core, 1, keepdims=False)
        return chosen.reshape(HEADS // 2, full.shape[1], full.shape[2])

    own = latent[0].T
    mate = lax.ppermute(own, "core", swap)
    prev_same = lax.ppermute(own, "x", [(i, i + 1) for i in range(NX - 1)])
    prev_mate = lax.ppermute(prev_same, "core", swap)
    q_full = query[0].transpose(1, 2, 0)
    q_got = lax.ppermute(q_full, "core", swap)
    g_full = tie(grad_out[0].transpose(1, 0, 2))
    g_got = lax.ppermute(other_half(g_full), "core", swap)

    core_info = core.astype(jnp.int32).reshape(1)
    lat, latt, rope = window_of(core_info, (own, mate, prev_same, prev_mate))
    base = x * CHIP
    starts = start_of(doc_lengths[0], base + jnp.arange(CHIP, dtype=jnp.int32))
    low = (starts - (base - CHIP)).astype(jnp.int32).reshape(1, CHIP)

    def main(held, *ahead):
        info = jnp.stack([core] + [lax.rem(x + n, NX) for n in ahead]).astype(jnp.int32)
        return main_groups(
            len(ahead), info, q_full, q_got, g_full, g_got, w_kv, lat, latt, rope, low, held
        )

    held, (dw_left, dw_right), part_0 = main((), 1, 3)
    from_left = lax.ppermute(dw_left, "x", ring(1))
    from_right = lax.ppermute(dw_right, "x", ring(3))
    held, (dw_far,), part_1 = main(held, 2)
    across = all_to_all(dw_far.reshape(NY * NZ, LAT, 128), ("y", "z"))
    (dq, send), (dw_own,), part_2 = main(held, 0)

    got = lax.ppermute(send, "core", swap)
    wide, narrow = fold((part_0, part_1, part_2))
    wide = wide.reshape(2, NCORE, LAT + ROPE, ROWS)
    narrow = narrow.reshape(2, NCORE, LAT + ROPE, ROWS)
    prev_sum, own_sum = lax.dynamic_index_in_dim(wide, core, 1, keepdims=False)
    give = lax.dynamic_index_in_dim(narrow, 1 - core, 1, keepdims=False)
    taken = lax.ppermute(give, "core", swap)
    prev_sum = (prev_sum + taken[0].astype(F32)).astype(BF16)
    d_query = place(core_info, got, dq)

    across = lax.ppermute(summed(across), "x", ring(2))
    mine = total([dw_own, from_left, from_right]).astype(BF16)
    mine = all_to_all(mine.reshape(NY * NZ, LAT, 128), ("y", "z"))
    from_next = lax.ppermute(prev_sum, "x", [(i + 1, i) for i in range(NX - 1)])
    d_latent = total([own_sum, taken[1], from_next]).astype(BF16).T
    d_weight = (jnp.sum(mine.astype(F32), axis=0) + across.astype(F32)).T

    return (d_query.transpose(2, 0, 1)[None], d_latent[None], d_weight)


def solution(mesh):
    fine = Mesh(mesh.devices.reshape(NX, NCORE, NY, NZ), ("x", "core", "y", "z"))
    dp, ctx = ("y", "z"), ("x", "core")
    in_specs = (P(dp, ctx, None, None), P(dp, ctx, None), P(dp, None), P(), P(dp, ctx, None, None))
    out_specs = (P(dp, ctx, None, None), P(dp, ctx, None), P(("x", "core", "y", "z"), None))
    return jax.shard_map(
        per_device, mesh=fine, in_specs=in_specs, out_specs=out_specs, check_vma=False
    )
```

```python
import functools
import math

import jax
import jax.numpy as jnp
from jax import lax
from jax.experimental import pallas as pl
from jax.experimental.pallas import tpu as pltpu
from jax.sharding import Mesh
from jax.sharding import PartitionSpec as P

F32 = jnp.float32
BF16 = jnp.bfloat16
NX, NCORE, NY, NZ = 4, 2, 4, 4
HEADS = 64
NOPE = 128
ROPE = 64
WIDTH = NOPE + ROPE
VDIM = 128
HCOLS = NOPE + VDIM
LAT = 512
ROWS = 128
CHIP = NCORE * ROWS
KEYS = 2 * CHIP
GROUP = 8
PER_STEP = 4
STEPS = GROUP // PER_STEP
SCALE = 1.0 / math.sqrt(WIDTH)
LOG2E = math.log2(math.e)
NT = (((1,), (1,)), ((), ()))
TN = (((0,), (0,)), ((), ()))


def mm(a, b, dims=(((1,), (0,)), ((), ()))):
    return lax.dot_general(a, b, dims, preferred_element_type=F32)


def main_kernel(groups, info, *refs):
    q_own, q_got, g_own, g_got, w_ref, lat_ref, latt_ref, rope_ref, low_ref = refs[:9]
    dlat_ref, drope_ref, bias_ref = refs[-3:]
    dw_refs = refs[-3 - groups : -3]
    dq_ref, send_ref = refs[-5 - groups : -3 - groups]
    first_core = info[0] == 0
    step = pl.program_id(0)

    @pl.when(step == 0)
    def _():
        key = lax.broadcasted_iota(jnp.int32, (KEYS, CHIP), 0)
        row = lax.broadcasted_iota(jnp.int32, (KEYS, CHIP), 1)
        ok = (key >= low_ref[...]) & (key <= row + CHIP)
        bias_ref[...] = jnp.where(ok, 0.0, -1e30)
        dlat_ref[...] = jnp.zeros_like(dlat_ref)
        drope_ref[...] = jnp.zeros_like(drope_ref)

    rope = rope_ref[...]
    kv_all = mm(lat_ref[...], w_ref[...], NT).astype(BF16)
    fronts = []
    for i in range(PER_STEP):
        qo, qr, go, gr = q_own[i], q_got[i], g_own[i], g_got[i]
        q = jnp.concatenate([jnp.where(first_core, qo, qr), jnp.where(first_core, qr, qo)], axis=1)
        g = jnp.concatenate([jnp.where(first_core, go, gr), jnp.where(first_core, gr, go)], axis=0)
        col = i * HCOLS
        k = jnp.concatenate([kv_all[:, col : col + NOPE], rope], axis=1)
        v = kv_all[:, col + NOPE : col + HCOLS]
        s = mm(k, q) * (SCALE * LOG2E) + bias_ref[...]
        dp = mm(v, g, NT)
        e = jnp.exp2(s - jnp.max(s, axis=0, keepdims=True))
        r = 1.0 / jnp.sum(e, axis=0, keepdims=True)
        delta = jnp.sum(e * dp, axis=0, keepdims=True) * r
        rs = r * SCALE
        ds = (e * (dp * rs - delta * rs)).astype(BF16)
        fronts.append((q, g, k, ds, (e * r).astype(BF16)))
    dkvs, dropes = [], []
    for i, (q, g, k, ds, p) in enumerate(fronts):
        dq = mm(k, ds, TN).astype(BF16)
        dq_ref[i] = jnp.where(first_core, dq[:, :ROWS], dq[:, ROWS:])
        send_ref[i] = jnp.where(first_core, dq[:, ROWS:], dq[:, :ROWS])
        dk = mm(ds, q, NT)
        dv = mm(p, g)
        dropes.append(dk[:, NOPE:])
        dkvs.append(jnp.concatenate([dk[:, :NOPE], dv], axis=1).astype(BF16))
    drope_ref[...] += functools.reduce(jnp.add, dropes)
    dkv = jnp.concatenate(dkvs, axis=1)
    dw = mm(latt_ref[...], dkv).astype(BF16)
    for group, dw_ref in enumerate(dw_refs):

        @pl.when(step // STEPS == group)
        def _():
            for j in range(2 * PER_STEP):
                dw_ref[j // NZ, j % NZ] = dw[:, j * 128 : (j + 1) * 128]

    dlat_ref[...] += mm(dkv, w_ref[...])


def main_groups(groups, info, q_full, q_got, g_full, g_got, w_kv, lat, latt, rope, low, held):
    group_of = lambda i, info: info[1 + i // STEPS]
    half = lambda i, info: (group_of(i, info) * STEPS + i % STEPS, 0, 0)
    full = lambda i, info: ((2 * group_of(i, info) + info[0]) * STEPS + i % STEPS, 0, 0)
    w_rows = lambda i, info: ((2 * group_of(i, info) + info[0]) * STEPS + i % STEPS, 0)
    whole = lambda i, info: (0, 0)
    ys = 2 * PER_STEP // NZ

    def dw_spec(group):
        def index(i, info):
            return (jnp.clip(i - group * STEPS, 0, STEPS - 1), 0, 0, 0)

        return pl.BlockSpec((ys, NZ, LAT, 128), index)

    in_specs = [
        pl.BlockSpec((PER_STEP, WIDTH, ROWS), full),
        pl.BlockSpec((PER_STEP, WIDTH, ROWS), full),
        pl.BlockSpec((PER_STEP, ROWS, VDIM), full),
        pl.BlockSpec((PER_STEP, ROWS, VDIM), half),
        pl.BlockSpec((PER_STEP * HCOLS, LAT), w_rows),
        pl.BlockSpec((KEYS, LAT), whole),
        pl.BlockSpec((LAT, KEYS), whole),
        pl.BlockSpec((KEYS, ROPE), whole),
        pl.BlockSpec((1, CHIP), whole),
    ]
    aliases = {}
    if held:
        in_specs += [pl.BlockSpec(memory_space=pl.ANY)] * 2
        aliases = {10: 0, 11: 1}
    grid_spec = pltpu.PrefetchScalarGridSpec(
        num_scalar_prefetch=1,
        grid=(groups * STEPS,),
        in_specs=in_specs,
        out_specs=[
            pl.BlockSpec((PER_STEP, WIDTH, ROWS), full),
            pl.BlockSpec((PER_STEP, WIDTH, ROWS), half),
        ]
        + [dw_spec(group) for group in range(groups)]
        + [pl.BlockSpec((KEYS, LAT), whole), pl.BlockSpec((KEYS, ROPE), whole)],
        scratch_shapes=[pltpu.VMEM((KEYS, CHIP), F32)],
    )
    outs = pl.pallas_call(
        functools.partial(main_kernel, groups),
        grid_spec=grid_spec,
        out_shape=[
            pltpu.HBM((HEADS, WIDTH, ROWS), BF16),
            pltpu.HBM((HEADS // 2, WIDTH, ROWS), BF16),
        ]
        + [pltpu.HBM((NY, NZ, LAT, 128), BF16)] * groups
        + [pltpu.HBM((KEYS, LAT), F32), pltpu.HBM((KEYS, ROPE), F32)],
        input_output_aliases=aliases,
        compiler_params=pltpu.CompilerParams(
            dimension_semantics=("arbitrary",), vmem_limit_bytes=48 * 1024 * 1024
        ),
        cost_estimate=pl.CostEstimate(
            flops=0, bytes_accessed=0, transcendentals=0
        ),
        name="main_groups",
    )(info, q_full, q_got, g_full, g_got, w_kv, lat, latt, rope, low, *held)
    return tuple(outs[:2]), outs[2 : 2 + groups], (outs[-2], outs[-1])


def fold_kernel(*refs):
    parts, (wide_ref, narrow_ref) = refs[:-2], refs[-2:]
    dlat = functools.reduce(jnp.add, [ref[...] for ref in parts[0::2]])
    drope = functools.reduce(jnp.add, [ref[...] for ref in parts[1::2]])
    block = jnp.concatenate([dlat.T, drope.T], axis=0)
    wide_ref[0] = block
    narrow_ref[0] = block.astype(BF16)


def fold(parts):
    width = LAT + ROPE
    rows = lambda j: (j, 0)
    out = pl.BlockSpec((1, width, ROWS), lambda j: (j, 0, 0))
    return pl.pallas_call(
        fold_kernel,
        grid=(KEYS // ROWS,),
        in_specs=[pl.BlockSpec((ROWS, LAT), rows), pl.BlockSpec((ROWS, ROPE), rows)] * len(parts),
        out_specs=[out, out],
        out_shape=[
            jax.ShapeDtypeStruct((4, width, ROWS), F32),
            jax.ShapeDtypeStruct((4, width, ROWS), BF16),
        ],
        compiler_params=pltpu.CompilerParams(dimension_semantics=("arbitrary",)),
        cost_estimate=pl.CostEstimate(flops=0, bytes_accessed=0, transcendentals=0),
        name="fold",
    )(*[array for pair in parts for array in pair])


def window_kernel(info, own, mate, prev_same, prev_mate, lat_ref, latt_ref, rope_ref):
    first_core = info[0] == 0

    def pair(mine, other):
        return [jnp.where(first_core, mine, other), jnp.where(first_core, other, mine)]

    window = jnp.concatenate(
        pair(prev_same[...], prev_mate[...]) + pair(own[...], mate[...]), axis=1
    )
    latt_ref[...] = window[:LAT]
    lat_ref[...] = window[:LAT].T
    rope_ref[...] = window[LAT:].T


def window_of(info, pieces):
    return pl.pallas_call(
        window_kernel,
        in_specs=[pl.BlockSpec(memory_space=pltpu.SMEM)]
        + [pl.BlockSpec(memory_space=pltpu.VMEM)] * 4,
        out_shape=[
            jax.ShapeDtypeStruct((KEYS, LAT), BF16),
            jax.ShapeDtypeStruct((LAT, KEYS), BF16),
            jax.ShapeDtypeStruct((KEYS, ROPE), BF16),
        ],
        compiler_params=pltpu.CompilerParams(vmem_limit_bytes=32 * 1024 * 1024),
        name="window",
    )(info, *pieces)


def place_kernel(info, got_ref, held_ref, out_ref):
    out_ref[...] = got_ref[...]


def place(info, got, held):
    block = (GROUP, WIDTH, ROWS)
    grid_spec = pltpu.PrefetchScalarGridSpec(
        num_scalar_prefetch=1,
        grid=(NX,),
        in_specs=[
            pl.BlockSpec(block, lambda i, info: (i, 0, 0)),
            pl.BlockSpec(memory_space=pl.ANY),
        ],
        out_specs=pl.BlockSpec(block, lambda i, info: (2 * i + 1 - info[0], 0, 0)),
    )
    return pl.pallas_call(
        place_kernel,
        grid_spec=grid_spec,
        out_shape=pltpu.HBM((HEADS, WIDTH, ROWS), BF16),
        input_output_aliases={2: 0},
        compiler_params=pltpu.CompilerParams(dimension_semantics=("arbitrary",)),
        cost_estimate=pl.CostEstimate(flops=0, bytes_accessed=0, transcendentals=0),
        name="place",
    )(info, got, held)


def start_of(lengths, positions):
    ends = jnp.cumsum(lengths)
    picked = jnp.where(ends[None, :] <= positions[:, None], lengths[None, :], 0)
    return jnp.sum(picked, axis=1)


def ring(distance):
    return [(i, (i + distance) % 4) for i in range(4)]


def pick(blocks, index):
    return lax.dynamic_index_in_dim(blocks, index, 0, keepdims=False)


def exchange(blocks, axis, me):
    got = [pick(blocks, me)]
    for distance in (1, 3, 2):
        sent = pick(blocks, lax.rem(me + distance, 4))
        got.append(lax.ppermute(sent, axis, ring(distance)))
    return got


def total(parts):
    return functools.reduce(jnp.add, [part.astype(F32) for part in parts])


def all_to_all(blocks, axis):
    return lax.all_to_all(blocks, axis, 0, 0, tiled=True)


def summed(parts):
    return jnp.sum(parts.astype(F32), axis=0).astype(BF16)


def per_device(query, latent, doc_lengths, w_kv, grad_out):
    x, core = lax.axis_index("x"), lax.axis_index("core")
    y, z = lax.axis_index("y"), lax.axis_index("z")
    swap = [(0, 1), (1, 0)]
    tie = lax.optimization_barrier

    def other_half(full):
        parts = full.reshape(NX, NCORE, GROUP, full.shape[1], full.shape[2])
        chosen = lax.dynamic_index_in_dim(parts, 1 - core, 1, keepdims=False)
        return chosen.reshape(HEADS // 2, full.shape[1], full.shape[2])

    own = latent[0].T
    mate = lax.ppermute(own, "core", swap)
    prev_same = lax.ppermute(own, "x", [(i, i + 1) for i in range(NX - 1)])
    q_full = query[0].transpose(1, 2, 0)
    q_got = lax.ppermute(q_full, "core", swap)
    g_full = tie(grad_out[0].transpose(1, 0, 2))
    prev_same, mate, g_full = tie((prev_same, mate, g_full))
    g_got = lax.ppermute(other_half(g_full), "core", swap)

    core_info = core.astype(jnp.int32).reshape(1)
    prev_mate = lax.ppermute(prev_same, "core", swap)
    lat, latt, rope = window_of(core_info, (own, mate, prev_same, prev_mate))
    base = x * CHIP
    starts = start_of(doc_lengths[0], base + jnp.arange(CHIP, dtype=jnp.int32))
    low = (starts - (base - CHIP)).astype(jnp.int32).reshape(1, CHIP)

    def main(held, *ahead):
        info = jnp.stack([core] + [lax.rem(x + n, NX) for n in ahead]).astype(jnp.int32)
        return main_groups(
            len(ahead), info, q_full, q_got, g_full, g_got, w_kv, lat, latt, rope, low, held
        )

    held, (dw_left, dw_right), part_0 = main((), 1, 3)
    from_left = lax.ppermute(dw_left, "x", ring(1))
    from_right = lax.ppermute(dw_right, "x", ring(3))
    held, (dw_far,), part_1 = main(held, 2)
    across = all_to_all(dw_far.reshape(NY * NZ, LAT, 128), ("y", "z"))
    (dq, send), (dw_own,), part_2 = main(held, 0)

    got = lax.ppermute(send, "core", swap)
    wide, narrow = fold((part_0, part_1, part_2))
    wide = wide.reshape(2, NCORE, LAT + ROPE, ROWS)
    narrow = narrow.reshape(2, NCORE, LAT + ROPE, ROWS)
    prev_sum, own_sum = lax.dynamic_index_in_dim(wide, core, 1, keepdims=False)
    give = lax.dynamic_index_in_dim(narrow, 1 - core, 1, keepdims=False)
    taken = lax.ppermute(give, "core", swap)
    prev_sum = (prev_sum + taken[0].astype(F32)).astype(BF16)
    d_query = place(core_info, got, dq)

    across = lax.ppermute(summed(across), "x", ring(2))
    mine = total([dw_own, from_left, from_right]).astype(BF16)
    mine = all_to_all(mine.reshape(NY * NZ, LAT, 128), ("y", "z"))
    from_next = lax.ppermute(prev_sum, "x", [(i + 1, i) for i in range(NX - 1)])
    d_latent = total([own_sum, taken[1], from_next]).astype(BF16).T
    d_weight = (jnp.sum(mine.astype(F32), axis=0) + across.astype(F32)).T

    return (d_query.transpose(2, 0, 1)[None], d_latent[None], d_weight)


def solution(mesh):
    fine = Mesh(mesh.devices.reshape(NX, NCORE, NY, NZ), ("x", "core", "y", "z"))
    dp, ctx = ("y", "z"), ("x", "core")
    in_specs = (P(dp, ctx, None, None), P(dp, ctx, None), P(dp, None), P(), P(dp, ctx, None, None))
    out_specs = (P(dp, ctx, None, None), P(dp, ctx, None), P(("x", "core", "y", "z"), None))
    return jax.shard_map(
        per_device, mesh=fine, in_specs=in_specs, out_specs=out_specs, check_vma=False
    )
```

```python
import functools
import math

import jax
import jax.numpy as jnp
from jax import lax
from jax.experimental import pallas as pl
from jax.experimental.pallas import tpu as pltpu
from jax.sharding import Mesh
from jax.sharding import PartitionSpec as P

F32 = jnp.float32
BF16 = jnp.bfloat16
NX, NCORE, NY, NZ = 4, 2, 4, 4
HEADS = 64
NOPE = 128
ROPE = 64
WIDTH = NOPE + ROPE
VDIM = 128
HCOLS = NOPE + VDIM
LAT = 512
ROWS = 128
CHIP = NCORE * ROWS
KEYS = 2 * CHIP
GROUP = 8
PER_STEP = 4
STEPS = GROUP // PER_STEP
SCALE = 1.0 / math.sqrt(WIDTH)
LOG2E = math.log2(math.e)
NT = (((1,), (1,)), ((), ()))
TN = (((0,), (0,)), ((), ()))


def in_hbm(array):
    return pltpu.with_memory_space_constraint(array, pltpu.HBM)


def mm(a, b, dims=(((1,), (0,)), ((), ()))):
    return lax.dot_general(a, b, dims, preferred_element_type=F32)


def main_kernel(groups, info, *refs):
    q_own, q_got, g_own, g_got, w_ref, lat_ref, latt_ref, rope_ref, low_ref = refs[:9]
    dlat_ref, drope_ref, bias_ref = refs[-3:]
    dw_refs = refs[-3 - groups : -3]
    dq_ref, send_ref = refs[-5 - groups : -3 - groups]
    first_core = info[0] == 0
    step = pl.program_id(0)

    @pl.when(step == 0)
    def _():
        key = lax.broadcasted_iota(jnp.int32, (KEYS, CHIP), 0)
        row = lax.broadcasted_iota(jnp.int32, (KEYS, CHIP), 1)
        ok = (key >= low_ref[...]) & (key <= row + CHIP)
        bias_ref[...] = jnp.where(ok, 0.0, -1e30)
        dlat_ref[...] = jnp.zeros_like(dlat_ref)
        drope_ref[...] = jnp.zeros_like(drope_ref)

    rope = rope_ref[...]
    kv_all = mm(lat_ref[...], w_ref[...], NT).astype(BF16)
    fronts = []
    for i in range(PER_STEP):
        qo, qr, go, gr = q_own[i], q_got[i], g_own[i], g_got[i]
        q = jnp.concatenate([jnp.where(first_core, qo, qr), jnp.where(first_core, qr, qo)], axis=1)
        g = jnp.concatenate([jnp.where(first_core, go, gr), jnp.where(first_core, gr, go)], axis=0)
        col = i * HCOLS
        k = jnp.concatenate([kv_all[:, col : col + NOPE], rope], axis=1)
        v = kv_all[:, col + NOPE : col + HCOLS]
        s = mm(k, q) * (SCALE * LOG2E) + bias_ref[...]
        dp = mm(v, g, NT)
        e = jnp.exp2(s - jnp.max(s, axis=0, keepdims=True))
        r = 1.0 / jnp.sum(e, axis=0, keepdims=True)
        delta = jnp.sum(e * dp, axis=0, keepdims=True) * r
        rs = r * SCALE
        ds = (e * (dp * rs - delta * rs)).astype(BF16)
        fronts.append((q, g, k, ds, (e * r).astype(BF16)))
    dkvs, dropes = [], []
    for i, (q, g, k, ds, p) in enumerate(fronts):
        dq = mm(k, ds, TN).astype(BF16)
        dq_ref[i] = jnp.where(first_core, dq[:, :ROWS], dq[:, ROWS:])
        send_ref[i] = jnp.where(first_core, dq[:, ROWS:], dq[:, :ROWS])
        dk = mm(ds, q, NT)
        dv = mm(p, g)
        dropes.append(dk[:, NOPE:])
        dkvs.append(jnp.concatenate([dk[:, :NOPE], dv], axis=1).astype(BF16))
    drope_ref[...] += functools.reduce(jnp.add, dropes)
    dkv = jnp.concatenate(dkvs, axis=1)
    dw = mm(latt_ref[...], dkv).astype(BF16)
    for group, dw_ref in enumerate(dw_refs):

        @pl.when(step // STEPS == group)
        def _():
            for j in range(2 * PER_STEP):
                dw_ref[j // NZ, j % NZ] = dw[:, j * 128 : (j + 1) * 128]

    dlat_ref[...] += mm(dkv, w_ref[...])


def main_groups(groups, info, q_full, q_got, g_full, g_got, w_kv, lat, latt, rope, low, held):
    group_of = lambda i, info: info[1 + i // STEPS]
    half = lambda i, info: (group_of(i, info) * STEPS + i % STEPS, 0, 0)
    full = lambda i, info: ((2 * group_of(i, info) + info[0]) * STEPS + i % STEPS, 0, 0)
    w_rows = lambda i, info: ((2 * group_of(i, info) + info[0]) * STEPS + i % STEPS, 0)
    whole = lambda i, info: (0, 0)
    ys = 2 * PER_STEP // NZ

    def dw_spec(group):
        def index(i, info):
            return (jnp.clip(i - group * STEPS, 0, STEPS - 1), 0, 0, 0)

        return pl.BlockSpec((ys, NZ, LAT, 128), index)

    in_specs = [
        pl.BlockSpec((PER_STEP, WIDTH, ROWS), full),
        pl.BlockSpec((PER_STEP, WIDTH, ROWS), full),
        pl.BlockSpec((PER_STEP, ROWS, VDIM), full),
        pl.BlockSpec((PER_STEP, ROWS, VDIM), half),
        pl.BlockSpec((PER_STEP * HCOLS, LAT), w_rows),
        pl.BlockSpec((KEYS, LAT), whole),
        pl.BlockSpec((LAT, KEYS), whole),
        pl.BlockSpec((KEYS, ROPE), whole),
        pl.BlockSpec((1, CHIP), whole),
    ]
    aliases = {}
    if held:
        in_specs += [pl.BlockSpec(memory_space=pl.ANY)] * 2
        aliases = {10: 0, 11: 1}
    grid_spec = pltpu.PrefetchScalarGridSpec(
        num_scalar_prefetch=1,
        grid=(groups * STEPS,),
        in_specs=in_specs,
        out_specs=[
            pl.BlockSpec((PER_STEP, WIDTH, ROWS), full),
            pl.BlockSpec((PER_STEP, WIDTH, ROWS), half),
        ]
        + [dw_spec(group) for group in range(groups)]
        + [pl.BlockSpec((KEYS, LAT), whole), pl.BlockSpec((KEYS, ROPE), whole)],
        scratch_shapes=[pltpu.VMEM((KEYS, CHIP), F32)],
    )
    outs = pl.pallas_call(
        functools.partial(main_kernel, groups),
        grid_spec=grid_spec,
        out_shape=[
            pltpu.HBM((HEADS, WIDTH, ROWS), BF16),
            pltpu.HBM((HEADS // 2, WIDTH, ROWS), BF16),
        ]
        + [pltpu.HBM((NY, NZ, LAT, 128), BF16)] * groups
        + [pltpu.HBM((KEYS, LAT), F32), pltpu.HBM((KEYS, ROPE), F32)],
        input_output_aliases=aliases,
        compiler_params=pltpu.CompilerParams(
            dimension_semantics=("arbitrary",), vmem_limit_bytes=48 * 1024 * 1024
        ),
        cost_estimate=pl.CostEstimate(
            flops=0, bytes_accessed=0, transcendentals=0
        ),
        name="main_groups",
    )(info, q_full, q_got, g_full, g_got, w_kv, in_hbm(lat), in_hbm(latt), rope, low, *held)
    return tuple(outs[:2]), outs[2 : 2 + groups], (outs[-2], outs[-1])


def fold_kernel(*refs):
    parts, (wide_ref, narrow_ref) = refs[:-2], refs[-2:]
    dlat = functools.reduce(jnp.add, [ref[...] for ref in parts[0::2]])
    drope = functools.reduce(jnp.add, [ref[...] for ref in parts[1::2]])
    block = jnp.concatenate([dlat.T, drope.T], axis=0)
    wide_ref[0] = block
    narrow_ref[0] = block.astype(BF16)


def fold(parts):
    width = LAT + ROPE
    rows = lambda j: (j, 0)
    out = pl.BlockSpec((1, width, ROWS), lambda j: (j, 0, 0))
    return pl.pallas_call(
        fold_kernel,
        grid=(KEYS // ROWS,),
        in_specs=[pl.BlockSpec((ROWS, LAT), rows), pl.BlockSpec((ROWS, ROPE), rows)] * len(parts),
        out_specs=[out, out],
        out_shape=[
            jax.ShapeDtypeStruct((4, width, ROWS), F32),
            jax.ShapeDtypeStruct((4, width, ROWS), BF16),
        ],
        compiler_params=pltpu.CompilerParams(dimension_semantics=("arbitrary",)),
        cost_estimate=pl.CostEstimate(flops=0, bytes_accessed=0, transcendentals=0),
        name="fold",
    )(*[array for pair in parts for array in pair])


def window_kernel(info, own, mate, prev_same, prev_mate, lat_ref, latt_ref, rope_ref):
    first_core = info[0] == 0

    def pair(mine, other):
        return [jnp.where(first_core, mine, other), jnp.where(first_core, other, mine)]

    window = jnp.concatenate(
        pair(prev_same[...], prev_mate[...]) + pair(own[...], mate[...]), axis=1
    )
    latt_ref[...] = window[:LAT]
    lat_ref[...] = window[:LAT].T
    rope_ref[...] = window[LAT:].T


def window_of(info, pieces):
    whole = lambda i, info: (0, 0)
    grid_spec = pltpu.PrefetchScalarGridSpec(
        num_scalar_prefetch=1,
        grid=(1,),
        in_specs=[pl.BlockSpec((LAT + ROPE, ROWS), whole)] * 4,
        out_specs=[
            pl.BlockSpec((KEYS, LAT), whole),
            pl.BlockSpec((LAT, KEYS), whole),
            pl.BlockSpec((KEYS, ROPE), whole),
        ],
    )
    return pl.pallas_call(
        window_kernel,
        grid_spec=grid_spec,
        out_shape=[
            pltpu.HBM((KEYS, LAT), BF16),
            pltpu.HBM((LAT, KEYS), BF16),
            jax.ShapeDtypeStruct((KEYS, ROPE), BF16),
        ],
        compiler_params=pltpu.CompilerParams(
            dimension_semantics=("arbitrary",), vmem_limit_bytes=32 * 1024 * 1024
        ),
        cost_estimate=pl.CostEstimate(flops=0, bytes_accessed=0, transcendentals=0),
        name="window",
    )(info, *[in_hbm(piece) for piece in pieces])


def place_kernel(info, got_ref, held_ref, out_ref):
    out_ref[...] = got_ref[...]


def place(info, got, held):
    block = (GROUP, WIDTH, ROWS)
    grid_spec = pltpu.PrefetchScalarGridSpec(
        num_scalar_prefetch=1,
        grid=(NX,),
        in_specs=[
            pl.BlockSpec(block, lambda i, info: (i, 0, 0)),
            pl.BlockSpec(memory_space=pl.ANY),
        ],
        out_specs=pl.BlockSpec(block, lambda i, info: (2 * i + 1 - info[0], 0, 0)),
    )
    return pl.pallas_call(
        place_kernel,
        grid_spec=grid_spec,
        out_shape=pltpu.HBM((HEADS, WIDTH, ROWS), BF16),
        input_output_aliases={2: 0},
        compiler_params=pltpu.CompilerParams(dimension_semantics=("arbitrary",)),
        cost_estimate=pl.CostEstimate(flops=0, bytes_accessed=0, transcendentals=0),
        name="place",
    )(info, got, held)


def start_of(lengths, positions):
    ends = jnp.cumsum(lengths)
    picked = jnp.where(ends[None, :] <= positions[:, None], lengths[None, :], 0)
    return jnp.sum(picked, axis=1)


def ring(distance):
    return [(i, (i + distance) % 4) for i in range(4)]


def pick(blocks, index):
    return lax.dynamic_index_in_dim(blocks, index, 0, keepdims=False)


def exchange(blocks, axis, me):
    got = [pick(blocks, me)]
    for distance in (1, 3, 2):
        sent = pick(blocks, lax.rem(me + distance, 4))
        got.append(lax.ppermute(sent, axis, ring(distance)))
    return got


def total(parts):
    return functools.reduce(jnp.add, [part.astype(F32) for part in parts])


def all_to_all(blocks, axis):
    return lax.all_to_all(blocks, axis, 0, 0, tiled=True)


def summed(parts):
    return jnp.sum(parts.astype(F32), axis=0).astype(BF16)


def per_device(query, latent, doc_lengths, w_kv, grad_out):
    x, core = lax.axis_index("x"), lax.axis_index("core")
    y, z = lax.axis_index("y"), lax.axis_index("z")
    swap = [(0, 1), (1, 0)]
    tie = lax.optimization_barrier

    def other_half(full):
        parts = full.reshape(NX, NCORE, GROUP, full.shape[1], full.shape[2])
        chosen = lax.dynamic_index_in_dim(parts, 1 - core, 1, keepdims=False)
        return chosen.reshape(HEADS // 2, full.shape[1], full.shape[2])

    own = latent[0].T
    mate = lax.ppermute(own, "core", swap)
    prev_same = lax.ppermute(own, "x", [(i, i + 1) for i in range(NX - 1)])
    q_full = query[0].transpose(1, 2, 0)
    q_got = lax.ppermute(q_full, "core", swap)
    g_full = tie(grad_out[0].transpose(1, 0, 2))
    prev_same, mate, g_full = tie((prev_same, mate, g_full))
    g_got = lax.ppermute(other_half(g_full), "core", swap)

    core_info = core.astype(jnp.int32).reshape(1)
    prev_mate = lax.ppermute(prev_same, "core", swap)
    lat, latt, rope = window_of(core_info, (own, mate, prev_same, prev_mate))
    base = x * CHIP
    starts = start_of(doc_lengths[0], base + jnp.arange(CHIP, dtype=jnp.int32))
    low = (starts - (base - CHIP)).astype(jnp.int32).reshape(1, CHIP)

    def main(held, *ahead):
        info = jnp.stack([core] + [lax.rem(x + n, NX) for n in ahead]).astype(jnp.int32)
        return main_groups(
            len(ahead), info, q_full, q_got, g_full, g_got, w_kv, lat, latt, rope, low, held
        )

    held, (dw_left, dw_right), part_0 = main((), 1, 3)
    from_left = lax.ppermute(dw_left, "x", ring(1))
    from_right = lax.ppermute(dw_right, "x", ring(3))
    held, (dw_far,), part_1 = main(held, 2)
    across = all_to_all(dw_far.reshape(NY * NZ, LAT, 128), ("y", "z"))
    (dq, send), (dw_own,), part_2 = main(held, 0)

    got = lax.ppermute(send, "core", swap)
    wide, narrow = fold((part_0, part_1, part_2))
    wide = wide.reshape(2, NCORE, LAT + ROPE, ROWS)
    narrow = narrow.reshape(2, NCORE, LAT + ROPE, ROWS)
    prev_sum, own_sum = lax.dynamic_index_in_dim(wide, core, 1, keepdims=False)
    give = lax.dynamic_index_in_dim(narrow, 1 - core, 1, keepdims=False)
    taken = lax.ppermute(give, "core", swap)
    prev_sum = (prev_sum + taken[0].astype(F32)).astype(BF16)
    d_query = place(core_info, got, dq)

    across = lax.ppermute(summed(across), "x", ring(2))
    mine = total([dw_own, from_left, from_right]).astype(BF16)
    mine = all_to_all(mine.reshape(NY * NZ, LAT, 128), ("y", "z"))
    from_next = lax.ppermute(prev_sum, "x", [(i + 1, i) for i in range(NX - 1)])
    d_latent = total([own_sum, taken[1], from_next]).astype(BF16).T
    d_weight = (jnp.sum(mine.astype(F32), axis=0) + across.astype(F32)).T

    return (d_query.transpose(2, 0, 1)[None], d_latent[None], d_weight)


def solution(mesh):
    fine = Mesh(mesh.devices.reshape(NX, NCORE, NY, NZ), ("x", "core", "y", "z"))
    dp, ctx = ("y", "z"), ("x", "core")
    in_specs = (P(dp, ctx, None, None), P(dp, ctx, None), P(dp, None), P(), P(dp, ctx, None, None))
    out_specs = (P(dp, ctx, None, None), P(dp, ctx, None), P(("x", "core", "y", "z"), None))
    return jax.shard_map(
        per_device, mesh=fine, in_specs=in_specs, out_specs=out_specs, check_vma=False
    )
```

```python
import functools
import math

import jax
import jax.numpy as jnp
from jax import lax
from jax.experimental import pallas as pl
from jax.experimental.pallas import tpu as pltpu
from jax.sharding import Mesh
from jax.sharding import PartitionSpec as P

F32 = jnp.float32
BF16 = jnp.bfloat16
NX, NCORE, NY, NZ = 4, 2, 4, 4
HEADS = 64
NOPE = 128
ROPE = 64
WIDTH = NOPE + ROPE
VDIM = 128
HCOLS = NOPE + VDIM
LAT = 512
ROWS = 128
CHIP = NCORE * ROWS
KEYS = 2 * CHIP
GROUP = 8
PER_STEP = 4
STEPS = GROUP // PER_STEP
SCALE = 1.0 / math.sqrt(WIDTH)
LOG2E = math.log2(math.e)
NT = (((1,), (1,)), ((), ()))
TN = (((0,), (0,)), ((), ()))


def in_hbm(array):
    return pltpu.with_memory_space_constraint(array, pltpu.HBM)


def mm(a, b, dims=(((1,), (0,)), ((), ()))):
    return lax.dot_general(a, b, dims, preferred_element_type=F32)


def main_kernel(groups, info, *refs):
    q_own, q_got, g_own, g_got, w_ref, lat_ref, latt_ref, rope_ref, low_ref = refs[:9]
    dlat_ref, drope_ref, bias_ref = refs[-3:]
    dw_refs = refs[-3 - groups : -3]
    dq_ref, send_ref = refs[-5 - groups : -3 - groups]
    first_core = info[0] == 0
    step = pl.program_id(0)

    @pl.when(step == 0)
    def _():
        key = lax.broadcasted_iota(jnp.int32, (KEYS, CHIP), 0)
        row = lax.broadcasted_iota(jnp.int32, (KEYS, CHIP), 1)
        ok = (key >= low_ref[...]) & (key <= row + CHIP)
        bias_ref[...] = jnp.where(ok, 0.0, -1e30)
        dlat_ref[...] = jnp.zeros_like(dlat_ref)
        drope_ref[...] = jnp.zeros_like(drope_ref)

    rope = rope_ref[...]
    kv_all = mm(lat_ref[...], w_ref[...], NT).astype(BF16)
    fronts = []
    for i in range(PER_STEP):
        qo, qr, go, gr = q_own[i], q_got[i], g_own[i], g_got[i]
        q = jnp.concatenate([jnp.where(first_core, qo, qr), jnp.where(first_core, qr, qo)], axis=1)
        g = jnp.concatenate([jnp.where(first_core, go, gr), jnp.where(first_core, gr, go)], axis=0)
        col = i * HCOLS
        k = jnp.concatenate([kv_all[:, col : col + NOPE], rope], axis=1)
        v = kv_all[:, col + NOPE : col + HCOLS]
        s = mm(k, q) * (SCALE * LOG2E) + bias_ref[...]
        dp = mm(v, g, NT)
        e = jnp.exp2(s - jnp.max(s, axis=0, keepdims=True))
        r = 1.0 / jnp.sum(e, axis=0, keepdims=True)
        delta = jnp.sum(e * dp, axis=0, keepdims=True) * r
        rs = r * SCALE
        ds = (e * (dp * rs - delta * rs)).astype(BF16)
        fronts.append((q, g, k, ds, (e * r).astype(BF16)))
    dkvs, dropes = [], []
    for i, (q, g, k, ds, p) in enumerate(fronts):
        dq = mm(k, ds, TN).astype(BF16)
        dq_ref[i] = jnp.where(first_core, dq[:, :ROWS], dq[:, ROWS:])
        send_ref[i] = jnp.where(first_core, dq[:, ROWS:], dq[:, :ROWS])
        dk = mm(ds, q, NT)
        dv = mm(p, g)
        dropes.append(dk[:, NOPE:])
        dkvs.append(jnp.concatenate([dk[:, :NOPE], dv], axis=1).astype(BF16))
    drope_ref[...] += functools.reduce(jnp.add, dropes)
    dkv = jnp.concatenate(dkvs, axis=1)
    dw = mm(latt_ref[...], dkv).astype(BF16)
    for group, dw_ref in enumerate(dw_refs):

        @pl.when(step // STEPS == group)
        def _():
            for j in range(2 * PER_STEP):
                dw_ref[j // NZ, j % NZ] = dw[:, j * 128 : (j + 1) * 128]

    dlat_ref[...] += mm(dkv, w_ref[...])


def main_groups(groups, info, q_full, q_got, g_full, g_got, w_kv, lat, latt, rope, low, held):
    group_of = lambda i, info: info[1 + i // STEPS]
    half = lambda i, info: (group_of(i, info) * STEPS + i % STEPS, 0, 0)
    full = lambda i, info: ((2 * group_of(i, info) + info[0]) * STEPS + i % STEPS, 0, 0)
    w_rows = lambda i, info: ((2 * group_of(i, info) + info[0]) * STEPS + i % STEPS, 0)
    whole = lambda i, info: (0, 0)
    ys = 2 * PER_STEP // NZ

    def dw_spec(group):
        def index(i, info):
            return (jnp.clip(i - group * STEPS, 0, STEPS - 1), 0, 0, 0)

        return pl.BlockSpec((ys, NZ, LAT, 128), index)

    in_specs = [
        pl.BlockSpec((PER_STEP, WIDTH, ROWS), full),
        pl.BlockSpec((PER_STEP, WIDTH, ROWS), full),
        pl.BlockSpec((PER_STEP, ROWS, VDIM), full),
        pl.BlockSpec((PER_STEP, ROWS, VDIM), half),
        pl.BlockSpec((PER_STEP * HCOLS, LAT), w_rows),
        pl.BlockSpec((KEYS, LAT), whole),
        pl.BlockSpec((LAT, KEYS), whole),
        pl.BlockSpec((KEYS, ROPE), whole),
        pl.BlockSpec((1, CHIP), whole),
    ]
    aliases = {}
    if held:
        in_specs += [pl.BlockSpec(memory_space=pl.ANY)] * 2
        aliases = {10: 0, 11: 1}
    grid_spec = pltpu.PrefetchScalarGridSpec(
        num_scalar_prefetch=1,
        grid=(groups * STEPS,),
        in_specs=in_specs,
        out_specs=[
            pl.BlockSpec((PER_STEP, WIDTH, ROWS), full),
            pl.BlockSpec((PER_STEP, WIDTH, ROWS), half),
        ]
        + [dw_spec(group) for group in range(groups)]
        + [pl.BlockSpec((KEYS, LAT), whole), pl.BlockSpec((KEYS, ROPE), whole)],
        scratch_shapes=[pltpu.VMEM((KEYS, CHIP), F32)],
    )
    outs = pl.pallas_call(
        functools.partial(main_kernel, groups),
        grid_spec=grid_spec,
        out_shape=[
            pltpu.HBM((HEADS, WIDTH, ROWS), BF16),
            pltpu.HBM((HEADS // 2, WIDTH, ROWS), BF16),
        ]
        + [pltpu.HBM((NY, NZ, LAT, 128), BF16)] * groups
        + [pltpu.HBM((KEYS, LAT), F32), pltpu.HBM((KEYS, ROPE), F32)],
        input_output_aliases=aliases,
        compiler_params=pltpu.CompilerParams(
            dimension_semantics=("arbitrary",), vmem_limit_bytes=48 * 1024 * 1024
        ),
        cost_estimate=pl.CostEstimate(
            flops=0, bytes_accessed=0, transcendentals=0
        ),
        name="main_groups",
    )(info, q_full, q_got, g_full, g_got, w_kv, in_hbm(lat), in_hbm(latt), rope, low, *held)
    return tuple(outs[:2]), outs[2 : 2 + groups], (outs[-2], outs[-1])


def fold_kernel(*refs):
    parts, (wide_ref, narrow_ref) = refs[:-2], refs[-2:]
    dlat = functools.reduce(jnp.add, [ref[...] for ref in parts[0::2]])
    drope = functools.reduce(jnp.add, [ref[...] for ref in parts[1::2]])
    block = jnp.concatenate([dlat.T, drope.T], axis=0)
    wide_ref[0] = block
    narrow_ref[0] = block.astype(BF16)


def fold(parts):
    width = LAT + ROPE
    rows = lambda j: (j, 0)
    out = pl.BlockSpec((1, width, ROWS), lambda j: (j, 0, 0))
    return pl.pallas_call(
        fold_kernel,
        grid=(KEYS // ROWS,),
        in_specs=[pl.BlockSpec((ROWS, LAT), rows), pl.BlockSpec((ROWS, ROPE), rows)] * len(parts),
        out_specs=[out, out],
        out_shape=[
            jax.ShapeDtypeStruct((4, width, ROWS), F32),
            jax.ShapeDtypeStruct((4, width, ROWS), BF16),
        ],
        compiler_params=pltpu.CompilerParams(dimension_semantics=("arbitrary",)),
        cost_estimate=pl.CostEstimate(flops=0, bytes_accessed=0, transcendentals=0),
        name="fold",
    )(*[array for pair in parts for array in pair])


def window_kernel(info, own, mate, prev_same, prev_mate, lat_ref, latt_ref, rope_ref):
    first_core = info[0] == 0

    def pair(mine, other):
        return [jnp.where(first_core, mine, other), jnp.where(first_core, other, mine)]

    window = jnp.concatenate(
        pair(prev_same[...], prev_mate[...]) + pair(own[...], mate[...]), axis=1
    )
    latt_ref[...] = window[:LAT]
    lat_ref[...] = window[:LAT].T
    rope_ref[...] = window[LAT:].T


def window_of(info, pieces):
    whole = lambda i, info: (0, 0)
    grid_spec = pltpu.PrefetchScalarGridSpec(
        num_scalar_prefetch=1,
        grid=(1,),
        in_specs=[pl.BlockSpec((LAT + ROPE, ROWS), whole)] * 4,
        out_specs=[
            pl.BlockSpec((KEYS, LAT), whole),
            pl.BlockSpec((LAT, KEYS), whole),
            pl.BlockSpec((KEYS, ROPE), whole),
        ],
    )
    return pl.pallas_call(
        window_kernel,
        grid_spec=grid_spec,
        out_shape=[
            pltpu.HBM((KEYS, LAT), BF16),
            pltpu.HBM((LAT, KEYS), BF16),
            jax.ShapeDtypeStruct((KEYS, ROPE), BF16),
        ],
        compiler_params=pltpu.CompilerParams(
            dimension_semantics=("arbitrary",), vmem_limit_bytes=32 * 1024 * 1024
        ),
        cost_estimate=pl.CostEstimate(flops=0, bytes_accessed=0, transcendentals=0),
        name="window",
    )(info, *[in_hbm(piece) for piece in pieces])


def place_kernel(info, got_ref, held_ref, out_ref):
    out_ref[...] = got_ref[...]


def place(info, got, held):
    block = (GROUP, WIDTH, ROWS)
    grid_spec = pltpu.PrefetchScalarGridSpec(
        num_scalar_prefetch=1,
        grid=(NX,),
        in_specs=[
            pl.BlockSpec(block, lambda i, info: (i, 0, 0)),
            pl.BlockSpec(memory_space=pl.ANY),
        ],
        out_specs=pl.BlockSpec(block, lambda i, info: (2 * i + 1 - info[0], 0, 0)),
    )
    return pl.pallas_call(
        place_kernel,
        grid_spec=grid_spec,
        out_shape=pltpu.HBM((HEADS, WIDTH, ROWS), BF16),
        input_output_aliases={2: 0},
        compiler_params=pltpu.CompilerParams(dimension_semantics=("arbitrary",)),
        cost_estimate=pl.CostEstimate(flops=0, bytes_accessed=0, transcendentals=0),
        name="place",
    )(info, got, held)


def start_of(lengths, positions):
    ends = jnp.cumsum(lengths)
    picked = jnp.where(ends[None, :] <= positions[:, None], lengths[None, :], 0)
    return jnp.sum(picked, axis=1)


def ring(distance):
    return [(i, (i + distance) % 4) for i in range(4)]


def pick(blocks, index):
    return lax.dynamic_index_in_dim(blocks, index, 0, keepdims=False)


def exchange(blocks, axis, me):
    got = [pick(blocks, me)]
    for distance in (1, 3, 2):
        sent = pick(blocks, lax.rem(me + distance, 4))
        got.append(lax.ppermute(sent, axis, ring(distance)))
    return got


def total(parts):
    return functools.reduce(jnp.add, [part.astype(F32) for part in parts])


def all_to_all(blocks, axis):
    return lax.all_to_all(blocks, axis, 0, 0, tiled=True)


def summed(parts):
    return jnp.sum(parts.astype(F32), axis=0).astype(BF16)


def per_device(query, latent, doc_lengths, w_kv, grad_out):
    x, core = lax.axis_index("x"), lax.axis_index("core")
    y, z = lax.axis_index("y"), lax.axis_index("z")
    swap = [(0, 1), (1, 0)]
    tie = lax.optimization_barrier

    def other_half(full):
        parts = full.reshape(NX, NCORE, GROUP, full.shape[1], full.shape[2])
        chosen = lax.dynamic_index_in_dim(parts, 1 - core, 1, keepdims=False)
        return chosen.reshape(HEADS // 2, full.shape[1], full.shape[2])

    own = latent[0].T
    mate = lax.ppermute(own, "core", swap)
    prev_same = lax.ppermute(own, "x", [(i, i + 1) for i in range(NX - 1)])
    q_full = query[0].transpose(1, 2, 0)
    q_got = lax.ppermute(q_full, "core", swap)
    g_full = tie(grad_out[0].transpose(1, 0, 2))
    prev_same, mate, g_full = tie((prev_same, mate, g_full))
    g_got = lax.ppermute(other_half(g_full), "core", swap)

    core_info = core.astype(jnp.int32).reshape(1)
    prev_mate = lax.ppermute(prev_same, "core", swap)
    lat, latt, rope = window_of(core_info, (own, mate, prev_same, prev_mate))
    base = x * CHIP
    starts = start_of(doc_lengths[0], base + jnp.arange(CHIP, dtype=jnp.int32))
    low = (starts - (base - CHIP)).astype(jnp.int32).reshape(1, CHIP)

    def main(held, *ahead):
        info = jnp.stack([core] + [lax.rem(x + n, NX) for n in ahead]).astype(jnp.int32)
        return main_groups(
            len(ahead), info, q_full, q_got, g_full, g_got, w_kv, lat, latt, rope, low, held
        )

    held, (dw_left, dw_right), part_0 = main((), 1, 3)
    from_left = lax.ppermute(dw_left, "x", ring(1))
    from_right = lax.ppermute(dw_right, "x", ring(3))
    held, (dw_far,), part_1 = main(held, 2)
    across = all_to_all(dw_far.reshape(NY * NZ, LAT, 128), ("y", "z"))
    (dq, send), (dw_own,), part_2 = main(held, 0)

    got = lax.ppermute(send, "core", swap)
    wide, narrow = fold((part_0, part_1, part_2))
    wide = wide.reshape(2, NCORE, LAT + ROPE, ROWS)
    narrow = narrow.reshape(2, NCORE, LAT + ROPE, ROWS)
    prev_sum, own_sum = lax.dynamic_index_in_dim(wide, core, 1, keepdims=False)
    give = lax.dynamic_index_in_dim(narrow, 1 - core, 1, keepdims=False)
    taken = lax.ppermute(give, "core", swap)
    prev_sum = (prev_sum + taken[0].astype(F32)).astype(BF16)
    d_query = place(core_info, got, dq)

    across = lax.ppermute(summed(across), "x", ring(2))
    mine = dw_own + (from_left + from_right)
    mine = all_to_all(mine.reshape(NY * NZ, LAT, 128), ("y", "z"))
    from_next = lax.ppermute(prev_sum, "x", [(i + 1, i) for i in range(NX - 1)])
    d_latent = total([own_sum, taken[1], from_next]).astype(BF16).T
    d_weight = (jnp.sum(mine.astype(F32), axis=0) + across.astype(F32)).T

    return (d_query.transpose(2, 0, 1)[None], d_latent[None], d_weight)


def solution(mesh):
    fine = Mesh(mesh.devices.reshape(NX, NCORE, NY, NZ), ("x", "core", "y", "z"))
    dp, ctx = ("y", "z"), ("x", "core")
    in_specs = (P(dp, ctx, None, None), P(dp, ctx, None), P(dp, None), P(), P(dp, ctx, None, None))
    out_specs = (P(dp, ctx, None, None), P(dp, ctx, None), P(("x", "core", "y", "z"), None))
    return jax.shard_map(
        per_device, mesh=fine, in_specs=in_specs, out_specs=out_specs, check_vma=False
    )
```
